256 devices in a mesh: dp: 2 (over y_lo), head: 16 (over z, core), blk: 8 (over y_hi, x).
Axes of the slice: x: 4, y: 4 (y_hi: 2, y_lo: 2; y = y_hi * 2 + y_lo), z: 8, core: 2. Of those that a mesh axis runs over, the one named last changes fastest.
Arguments:
- tokens: bfloat16 [2, 8192, 1024], P('dp', ('head', 'blk')), may hold values from -30 to 30
- cotangent: bfloat16 [2, 8192, 1024], P('dp', ('head', 'blk')), may hold values from -6 to 6
- qkv_weight: bfloat16 [3, 1024, 1024], P(None, 'head'), may hold values from -4 to 4
- out_weight: bfloat16 [1024, 1024], P('head'), may hold values from -0.1875 to 0.1875
- out_bias: float32 [1024], replicated, may hold values from -3 to 3
- norm_gain_vector: float32 [1024], replicated, may hold values from 0.1 to 1.9
- norm_bias_vector: float32 [1024], replicated, may hold values from -3 to 3
Outputs:
- layer_out: bfloat16 [2, 8192, 1024], P('dp', ('head', 'blk'))
- tokens_grad: bfloat16 [2, 8192, 1024], P('dp', ('head', 'blk'))
- qkv_grad: float32 [3, 1024, 1024], P(None, 'head')
- out_grad: float32 [1024, 1024], P('head')
- bias_grad: float32 [1024], replicated
- gain_grad: float32 [1024], replicated
- shift_grad: float32 [1024], replicated
The draws below stay inside these ranges and needn't reach their ends.
All inputs are finite; a program needn't handle non-finite values.
Results may differ from the reference program's by a relative error of at most 0.04.
Values may be sent and summed in bfloat16 or wider, within the bound.
No kernel may reach another device: no remote copies, remote signals or barrier semaphores. Data moves between devices by JAX's collectives and lax.ppermute only.
A program may use at most 128 MiB of HBM per device.

```python
import math
import jax
import jax.numpy as jnp
from jax import lax

D = 1024
HEADS = 16
IMAGES = 2
TOKENS = 8192


def draw_tokens(key, part):
    key = jax.random.fold_in(key, 11)
    first_key, second_key, third_key, fourth_key = jax.random.split(key, 4)
    spread = jnp.exp(jax.random.uniform(first_key, (IMAGES, TOKENS, 1), jnp.float32, jnp.log(0.5), jnp.log(5.0)))
    offset = 0.5 * jax.random.truncated_normal(second_key, -4.0, 4.0, (IMAGES, TOKENS, 1), jnp.float32)
    phases = jax.random.uniform(fourth_key, (IMAGES, 1, D), jnp.float32, -3.14159, 3.14159)
    position = jnp.arange(TOKENS, dtype=jnp.float32)[None, :, None] * (6.2831853 / TOKENS)
    pattern = 1.5 * jnp.cos(position + phases)
    base_values = jax.random.truncated_normal(third_key, -4.0, 4.0, (IMAGES, TOKENS, D), jnp.float32)
    return ((base_values + pattern) * spread + offset).astype(jnp.bfloat16)


def draw_qkv_weight(key, part):
    key = jax.random.fold_in(key, 23)
    first_key = jax.random.fold_in(key, 0)
    base_values = jax.random.truncated_normal(first_key, -4.0, 4.0, (3, D, D), jnp.float32) * D ** (-0.5)
    return base_values.astype(jnp.bfloat16)


def shard_levels(stream_key, shape, cuts, least, top_value):
    def one(dim, shards_of):
        heights = jax.random.uniform(jax.random.fold_in(jax.random.fold_in(stream_key, 6), dim), (shards_of,), jnp.float32, least / len(cuts), top_value / len(cuts))
        return jnp.repeat(jnp.exp(heights), shape[dim] // shards_of).reshape((-1,) + (1,) * (len(shape) - dim - 1))

    loudness = one(*cuts[0])
    for cut in cuts[1:]:
        loudness = loudness * one(*cut)
    return loudness


def bell_draw(key, dims, scale, bound, cuts=(), kind=jnp.bfloat16):
    drawn = scale * jax.random.normal(key, dims, jnp.float32)
    if cuts:
        drawn = drawn * shard_levels(key, dims, cuts, -0.22, 0.18)
    return jnp.clip(drawn, -bound, bound).astype(kind)


def setup_inputs(seed: int = 0) -> dict:
    arg_keys = jax.random.split(jax.random.key(seed), 8)
    tokens = draw_tokens(jax.random.fold_in(arg_keys[7], 71), 0)
    cotangent = bell_draw(arg_keys[1], (IMAGES, TOKENS, D), 1.0, 6.0, ((0, 2), (1, 128)))
    qkv_weight = draw_qkv_weight(jax.random.fold_in(arg_keys[7], 71), 0)
    out_weight = bell_draw(arg_keys[3], (D, D), D ** -0.5, 0.1875, ((0, 16),))
    out_bias = bell_draw(arg_keys[4], (D,), 0.5, 3.0, (), jnp.float32)
    norm_gain_vector = jnp.clip(1.0 + 0.18 * jax.random.normal(arg_keys[5], (D,), jnp.float32), 0.1, 1.9)
    norm_bias_vector = bell_draw(arg_keys[6], (D,), 0.5, 3.0, (), jnp.float32)
    return dict(tokens=tokens, cotangent=cotangent, qkv_weight=qkv_weight, out_weight=out_weight, out_bias=out_bias, norm_gain_vector=norm_gain_vector, norm_bias_vector=norm_bias_vector)


EPSILON = 1e-06

def apply_layer_norm(rows_in):
    values = rows_in.astype(jnp.float32)
    centre = lax.optimization_barrier(jnp.mean(values, axis=-1, keepdims=True))
    shifted = values - centre
    spread = lax.optimization_barrier(jnp.mean(shifted * shifted, axis=-1, keepdims=True))
    inverse_spread = lax.rsqrt(spread + EPSILON)
    return (shifted * inverse_spread, inverse_spread)

def head_pass(inputs):
    queries, key_rows, value_rows, grad_rows = inputs
    length, head_dim = queries.shape
    score_scale = 1.0 / math.sqrt(head_dim)
    block_size = math.gcd(1024, length)

    def one_block(carried, block_index):
        key_acc, value_acc = carried
        query_block = lax.dynamic_slice_in_dim(queries, block_index * block_size, block_size, 0)
        grad_block = lax.dynamic_slice_in_dim(grad_rows, block_index * block_size, block_size, 0)
        scores = jnp.dot(query_block, key_rows.T, preferred_element_type=jnp.float32) * score_scale
        row_max = lax.optimization_barrier(jnp.max(scores, axis=-1, keepdims=True))
        probabilities = jnp.exp(scores - row_max)
        row_total = lax.optimization_barrier(jnp.sum(probabilities, axis=-1, keepdims=True))
        log_total = row_max + jnp.log(row_total)
        weights = probabilities.astype(jnp.bfloat16)
        attended = (jnp.dot(weights, value_rows, preferred_element_type=jnp.float32) / row_total).astype(jnp.bfloat16)
        row_delta = lax.optimization_barrier(jnp.sum(grad_block.astype(jnp.float32) * attended.astype(jnp.float32), axis=-1, keepdims=True))
        back_probs = jnp.exp(scores - log_total)
        back_weights = back_probs.astype(jnp.bfloat16)
        value_acc = value_acc + jnp.dot(back_weights.T, grad_block, preferred_element_type=jnp.float32)
        prob_grad = jnp.dot(grad_block, value_rows.T, preferred_element_type=jnp.float32)
        score_grad = (back_probs * (prob_grad - row_delta)).astype(jnp.bfloat16)
        query_grad = jnp.dot(score_grad, key_rows, preferred_element_type=jnp.float32) * score_scale
        key_acc = key_acc + jnp.dot(score_grad.T, query_block, preferred_element_type=jnp.float32) * score_scale
        return ((key_acc, value_acc), (attended, query_grad))
    zero_rows = jnp.zeros((length, head_dim), jnp.float32)
    steps_all = jnp.arange(length // block_size, dtype=jnp.int32)
    (key_acc, value_acc), (attended, query_grad) = lax.scan(one_block, (zero_rows, zero_rows), steps_all)
    return (attended.reshape(length, head_dim), query_grad.reshape(length, head_dim), key_acc, value_acc)

def reference(tokens, cotangent, qkv_weight, out_weight, out_bias, norm_gain_vector, norm_bias_vector):
    images, length, model_width = tokens.shape
    head_dim = model_width // HEADS
    weight_rows = qkv_weight.reshape(3 * model_width, model_width)
    factor = 1.0 / math.sqrt(images * length)
    qkv_total = jnp.zeros((3 * model_width, model_width), jnp.float32)
    out_total = jnp.zeros((model_width, model_width), jnp.float32)
    bias_total = jnp.zeros((model_width,), jnp.float32)
    gain_overall = jnp.zeros((model_width,), jnp.float32)
    shift_total = jnp.zeros((model_width,), jnp.float32)
    outputs = []
    gradient_list = []
    for image_index in range(images):
        token_matrix = tokens[image_index]
        cotangent_tokens = cotangent[image_index]
        standardized_input, inverse_spread = apply_layer_norm(token_matrix)
        norm_result = (standardized_input * norm_gain_vector + norm_bias_vector).astype(jnp.bfloat16)
        packed = jnp.dot(norm_result, weight_rows.T, preferred_element_type=jnp.float32).astype(jnp.bfloat16)
        per_head = jnp.transpose(packed.reshape(length, 3, HEADS, head_dim), (1, 2, 0, 3))
        grad_att = jnp.dot(cotangent_tokens, out_weight.T, preferred_element_type=jnp.float32).astype(jnp.bfloat16)
        grad_heads = jnp.transpose(grad_att.reshape(length, HEADS, head_dim), (1, 0, 2))
        attended, query_grad, key_grad, value_grad = lax.map(head_pass, (per_head[0], per_head[1], per_head[2], grad_heads))
        attended = jnp.transpose(attended, (1, 0, 2)).reshape(length, model_width)
        projected = jnp.dot(attended, out_weight, preferred_element_type=jnp.float32)
        outputs.append((token_matrix.astype(jnp.float32) + projected + out_bias).astype(jnp.bfloat16))
        stacked = jnp.stack([query_grad, key_grad, value_grad], 0)
        packed_grad = jnp.transpose(stacked, (2, 0, 1, 3)).reshape(length, 3 * model_width).astype(jnp.bfloat16)
        norm_result_gradient = jnp.dot(packed_grad, weight_rows, preferred_element_type=jnp.float32)
        scaled_result = norm_result_gradient * norm_gain_vector
        mean_simple_term = lax.optimization_barrier(jnp.mean(scaled_result, axis=-1, keepdims=True))
        mean_product_term = lax.optimization_barrier(jnp.mean(scaled_result * standardized_input, axis=-1, keepdims=True))
        gradient_list.append((cotangent_tokens.astype(jnp.float32) + inverse_spread * (scaled_result - mean_simple_term - standardized_input * mean_product_term)).astype(jnp.bfloat16))
        qkv_total = qkv_total + jnp.dot(packed_grad.T, norm_result, preferred_element_type=jnp.float32)
        out_total = out_total + jnp.dot(attended.T, cotangent_tokens, preferred_element_type=jnp.float32)
        bias_total = bias_total + lax.optimization_barrier(jnp.sum(cotangent_tokens.astype(jnp.float32), axis=0))
        gain_overall = gain_overall + lax.optimization_barrier(jnp.sum(norm_result_gradient * standardized_input, axis=0))
        shift_total = shift_total + lax.optimization_barrier(jnp.sum(norm_result_gradient, axis=0))
    qkv_out = (qkv_total * factor).reshape(3, model_width, model_width)
    return (jnp.stack(outputs), jnp.stack(gradient_list), qkv_out, out_total * factor, bias_total * factor, gain_overall * factor, shift_total * factor)
```

```python
import functools
import math

import jax
import jax.numpy as jnp
from jax import lax
from jax.experimental import pallas as pl
from jax.experimental.pallas import tpu as pltpu
from jax.sharding import PartitionSpec as P

HEADS = 16
EPSILON = 1e-06
ZN = 8
XN = 4
F32 = jnp.float32
BF16 = jnp.bfloat16
WHOLE = pl.BlockSpec(memory_space=pltpu.VMEM)
ANY = pl.BlockSpec(memory_space=pl.ANY)
NT = (((1,), (1,)), ((), ()))
TN = (((0,), (0,)), ((), ()))
NN = (((1,), (0,)), ((), ()))

OFFSETS = (1, 3, 2)


def dot(a, b, dims=NN):
    return lax.dot_general(a, b, dims, preferred_element_type=F32)


def params(mib, flops=0, moved=0, trans=0):
    return dict(
        compiler_params=pltpu.CompilerParams(vmem_limit_bytes=mib * 2**20),
        cost_estimate=pl.CostEstimate(flops=flops, bytes_accessed=moved, transcendentals=trans),
    )


def permute(value, axis, count, target):
    return lax.ppermute(value, axis, [(i, target(i)) for i in range(count)])


def along_z(value, steps):
    return permute(value, "head", HEADS, lambda h: ((h // 2 + steps) % ZN) * 2 + h % 2)


def to_sibling(value):
    return permute(value, "head", HEADS, lambda h: h ^ 1)


def to_pair(value):
    return permute(value, "head", HEADS, lambda h: h ^ 2)


def to_diagonal(value):
    return permute(value, "head", HEADS, lambda h: h ^ 3)


def along_x(value, steps):
    return permute(value, "blk", 2 * XN, lambda b: (b // XN) * XN + (b % XN + steps) % XN)


def to_half(value):
    return permute(value, "blk", 2 * XN, lambda b: b ^ XN)


def unfold(pack):
    width = pack.shape[1] // 2
    return jnp.concatenate([pack[:, :width], pack[:, width:]], 0)


def fold(rows):
    half = rows.shape[0] // 2
    return jnp.concatenate([rows[:half], rows[half:]], 1)


def position():
    head = lax.axis_index("head")
    return head // 2, lax.rem(head, 2)


def normalise(rows):
    values = rows.astype(F32)
    shifted = values - jnp.mean(values, axis=-1, keepdims=True)
    spread = jnp.mean(shifted * shifted, axis=-1, keepdims=True)
    inverse = lax.rsqrt(spread + EPSILON)
    return shifted * inverse, inverse


def project_kernel(table, chained, *refs):
    count = len(table)
    pieces = refs[:count]
    weight, gain, bias = refs[count : count + 3]
    refs = refs[count + 3 + (3 if chained else 0) :]
    xhat_out, q_out, kv_out, normed = refs[0], refs[1], refs[2], refs[-1]
    z, core = position()
    width = q_out.shape[1]
    places, first = [], 0
    for n, (steps, flip, skip) in enumerate(table):
        own = core if flip == 0 else 1 - core
        start = lax.rem(z + steps + ZN, ZN) * 128 + own * 64 + skip
        start = pl.multiple_of(start, 32)
        height = pieces[n].shape[0]
        xhat, _ = normalise(pieces[n][...])
        xhat_out[pl.ds(start, height), :] = xhat.astype(BF16)
        normed[pl.ds(first, height), :] = (xhat * gain[...] + bias[...]).astype(BF16)
        places.append((pl.ds(start, height), first, first + height))
        first += height
    packed = dot(normed[...], weight[...], NT)
    queries = packed[:, :width].astype(BF16).astype(F32) * (1.0 / math.sqrt(width))
    queries = queries.astype(BF16)
    pairs = packed[:, width:].astype(BF16)
    for there, first, last in places:
        q_out[there, :] = queries[first:last]
        kv_out[there, :] = pairs[first:last]
    if chained:
        refs[3][...] = fold(q_out[...])


def project(table, pieces, weight, gain, bias, width, rows, before):
    total = sum(p.shape[0] for p in pieces)
    model = weight.shape[1]
    chained = [] if before is None else list(before)
    first = 3 + len(pieces)
    return pl.pallas_call(
        functools.partial(project_kernel, table, before is not None),
        out_shape=(
            jax.ShapeDtypeStruct((rows, model), BF16),
            jax.ShapeDtypeStruct((rows, width), BF16),
            jax.ShapeDtypeStruct((rows, 2 * width), BF16),
        )
        + ((jax.ShapeDtypeStruct((rows // 2, 2 * width), BF16),) if chained else ()),
        in_specs=[WHOLE] * (len(pieces) + 3 + len(chained)),
        out_specs=(WHOLE,) * (4 if chained else 3),
        scratch_shapes=[pltpu.VMEM((total, model), BF16)],
        input_output_aliases={first + n: n for n in range(len(chained))},
        name="project",
        **params(12, 2 * total * model * 3 * width, 4 * total * model * 2),
    )(*pieces, weight, gain, bias, *chained)


def forward_kernel(count, first, *refs):
    blocks = refs[:count]
    q_ref = refs[count]
    rest = refs[count + 1 :]
    if first:
        top = total = part = None
    else:
        top, total, part = rest[0][...], rest[1][...], rest[2][...]
        rest = rest[3:]
    m_out, l_out, acc_out = rest[:3]
    p_out, step_out = rest[3 : 3 + count], rest[3 + count : 3 + 2 * count]
    queries = unfold(q_ref[...])
    width = queries.shape[1]
    for n in range(count):
        kv = blocks[n]
        scores = dot(kv[:, :width], queries, NT)
        new = jnp.max(scores, axis=0, keepdims=True)
        if top is not None:
            new = jnp.maximum(top, new)
        probs = jnp.exp(scores - new)
        weights = probs.astype(BF16)
        p_out[n][...] = weights
        step_out[n][...] = new
        sums = jnp.sum(probs, axis=0, keepdims=True)
        values = dot(kv[:, width:], weights, TN)
        if top is None:
            total, part = sums, values
        else:
            shrink = jnp.exp(top - new)
            total, part = total * shrink + sums, part * shrink + values
        top = new
    m_out[...], l_out[...], acc_out[...] = top, total, part


def forward(blocks, queries, state):
    count = len(blocks)
    rows, width = 2 * queries.shape[0], queries.shape[1] // 2
    keys = blocks[0].shape[0]
    first = state is None
    states = [(1, rows), (1, rows), (width, rows)]
    out = pl.pallas_call(
        functools.partial(forward_kernel, count, first),
        out_shape=[jax.ShapeDtypeStruct(s, F32) for s in states]
        + [jax.ShapeDtypeStruct((keys, rows), BF16)] * count
        + [jax.ShapeDtypeStruct((1, rows), F32)] * count,
        in_specs=[WHOLE] * (count + 1 + (0 if first else 3)),
        out_specs=[WHOLE] * (3 + 2 * count),
        name="forward",
        **params(
            24,
            count * 16 * rows * keys * width, count * 2 * rows * keys, count * rows * keys
        ),
    )(*blocks, queries, *([] if first else state))
    return out[:3], out[3 : 3 + count], out[3 + count :]


def grad_att_kernel(cot, weight, out, sums):
    out[...] = fold(dot(cot[...], weight[...], NT).astype(BF16))
    sums[...] = jnp.sum(cot[...].astype(F32), axis=0, keepdims=True)


def grad_att(cot, weight):
    return pl.pallas_call(
        grad_att_kernel,
        out_shape=(
            jax.ShapeDtypeStruct((cot.shape[0] // 2, 2 * weight.shape[0]), BF16),
            jax.ShapeDtypeStruct((1, cot.shape[1]), F32),
        ),
        in_specs=[WHOLE, WHOLE],
        out_specs=(WHOLE, WHOLE),
        name="grad_att",
        **params(16, 8 * cot.shape[0] * cot.shape[1] * 64, 2 * cot.size),
    )(cot, weight)


def split_thrice(value):
    high = value.astype(BF16).astype(F32)
    rest = value - high
    middle_part = rest.astype(BF16).astype(F32)
    return [high, middle_part, rest - middle_part]


def message_kernel(*refs):
    out = refs[6]
    rows = refs[0].shape[1]
    width = refs[2].shape[0]
    for n in range(2):
        top, total, part = refs[3 * n : 3 * n + 3]
        here = pl.ds(n * rows, rows)
        out[:width, here] = part[...].astype(BF16)
        coded = split_thrice(top[...]) + split_thrice(total[...])
        coded = jnp.concatenate(coded + [jnp.zeros((10, rows), F32)], 0)
        out[width:, here] = coded.astype(BF16)


def message(own, other):
    width, rows = own[2].shape
    return pl.pallas_call(
        message_kernel,
        out_shape=jax.ShapeDtypeStruct((width + 16, 2 * rows), BF16),
        in_specs=[WHOLE] * 6,
        out_specs=WHOLE,
        name="message",
        **params(8, 4 * rows * width, 12 * rows * width),
    )(*own, *other)


def middle_kernel(*refs):
    got, grads = refs[6], refs[7:9]
    att_t, lses, deltas = refs[9], refs[10:12], refs[12:14]
    pieces, att = refs[14:18], refs[18]
    rows = refs[0].shape[1]
    width = refs[2].shape[0]
    for n in range(2):
        top, total, part = (ref[...] for ref in refs[3 * n : 3 * n + 3])
        here = pl.ds((1 - n) * rows, rows)
        coded = got[width:, here].astype(F32)
        their_top = coded[0:1] + coded[1:2] + coded[2:3]
        their_total = coded[3:4] + coded[4:5] + coded[5:6]
        new = jnp.maximum(top, their_top)
        mine, theirs = jnp.exp(top - new), jnp.exp(their_top - new)
        total = total * mine + their_total * theirs
        part = part * mine + got[:width, here].astype(F32) * theirs
        lses[n][...] = new + jnp.log(total)
        attended = (part / total).astype(BF16)
        back = jnp.transpose(unfold(grads[n][...]).astype(F32), (1, 0))
        wide = attended.astype(F32)
        deltas[n][...] = jnp.sum(back * wide, axis=0, keepdims=True)
        if n == 0:
            att_t[...] = attended
            att[...] = jnp.transpose(wide, (1, 0)).astype(BF16)
            regroup(att, *pieces)


def middle(own, other, got, grads):
    width, rows = own[2].shape
    quarter = jax.ShapeDtypeStruct((rows // 4, width), BF16)
    row = jax.ShapeDtypeStruct((1, rows), F32)
    out = pl.pallas_call(
        middle_kernel,
        out_shape=(jax.ShapeDtypeStruct((width, rows), BF16),) + (row,) * 4 + (quarter,) * 4,
        in_specs=[WHOLE] * 9,
        out_specs=(WHOLE,) * 9,
        scratch_shapes=[pltpu.VMEM((rows, width), BF16)],
        name="middle",
        **params(16, 10 * rows * width, 8 * rows * width),
    )(*own, *other, got, *grads)
    return out[0], out[1:3], out[3:5], out[5:9]


def regroup(rows, kept, sib, pair, diag):
    z, core = position()
    group, parity = z // 2, lax.rem(z, 2)
    width = rows.shape[1]
    for r in range(ZN // 2):
        base = lax.rem(group + r, ZN // 2) * 256
        to = pl.ds(r * 64, 64)
        for target, dp, dc in ((kept, 0, 0), (sib, 0, 1), (pair, 1, 0), (diag, 1, 1)):
            p = parity if dp == 0 else 1 - parity
            c = core if dc == 0 else 1 - core
            at = pl.multiple_of(base + p * 128 + c * 64, 64)
            target[to, :width] = rows[pl.ds(at, 64), :]


def lay_kernel(kept, sib, pair, diag, *outs):
    width = kept.shape[1]
    for r in range(4):
        here = pl.ds(r * 64, 64)
        for n, piece in enumerate((kept, sib, pair, diag)):
            outs[r][:, n * width : (n + 1) * width] = piece[here, :]


def lay(pieces):
    rows, width = pieces[0].shape
    return pl.pallas_call(
        lay_kernel,
        out_shape=[jax.ShapeDtypeStruct((rows // 4, 4 * width), BF16)] * 4,
        in_specs=[WHOLE] * 4,
        out_specs=[WHOLE] * 4,
        name="lay",
        **params(16, 0, 16 * rows * width),
    )(*pieces)


def layer_kernel(tokens, bias, weight, *refs):
    pieces, out = refs[:4], refs[4]
    z, core = position()
    group, parity = z // 2, lax.rem(z, 2)
    total = tokens[...].astype(F32) + bias[...]
    for r in range(4):
        base = lax.rem(group - r + ZN // 2, ZN // 2) * 256
        held = []
        for dp, dc in ((0, 0), (0, 1), (1, 0), (1, 1)):
            p = parity if dp == 0 else 1 - parity
            c = core if dc == 0 else 1 - core
            at = pl.multiple_of(base + p * 128 + c * 64, 64)
            held.append(weight[pl.ds(at, 64), :])
        total += dot(pieces[r][...], jnp.concatenate(held, 0))
    out[...] = total.astype(BF16)


def layer(tokens, bias, weight, pieces):
    return pl.pallas_call(
        layer_kernel,
        out_shape=jax.ShapeDtypeStruct(tokens.shape, BF16),
        in_specs=[WHOLE] * 7,
        out_specs=WHOLE,
        name="layer",
        **params(16, 8 * tokens.size * 1024, 2 * weight.size),
    )(tokens, bias, weight, *pieces)


def backward_kernel(count, given, kv, *refs):
    stored, tops, qs, grads, lses, deltas = (refs[n * count : (n + 1) * count] for n in range(6))
    rest = refs[6 * count :]
    before = rest[:count] if given else None
    out, dqs = rest[-count - 1], rest[-count:]
    width = qs[0].shape[1] // 2
    tile = qs[0].shape[0]
    dk = dv = 0
    for n in range(count):
        factor = jnp.exp(tops[n][...] - lses[n][...])
        for t in range(2):
            here = pl.ds(t * tile, tile)
            lanes = pl.ds(t * width, width)
            q, grad = qs[n][:, lanes], grads[n][:, lanes]
            prob_grad = dot(kv[:, width:], grad, NT)
            probs = stored[n][:, here].astype(F32) * factor[:, t * tile : (t + 1) * tile]
            score_grad = (probs * (prob_grad - deltas[n][:, here])).astype(BF16)
            dv += dot(probs.astype(BF16), grad)
            dk += dot(score_grad, q)
            dq = dot(kv[:, :width], score_grad, TN)
            total = dq if before is None else before[n][:, here] + dq
            dqs[n][:, here] = total.astype(dqs[n].dtype)
    out[:, :width] = dk.astype(out.dtype)
    out[:, width:] = dv.astype(out.dtype)


def backward(kv, stored, tops, qs, grads, lses, deltas, dqs, kinds):
    count = len(qs)
    rows, width = 2 * qs[0].shape[0], qs[0].shape[1] // 2
    keys = kv.shape[0]
    given = [] if dqs is None else list(dqs)
    out = pl.pallas_call(
        functools.partial(backward_kernel, count, dqs is not None),
        out_shape=[jax.ShapeDtypeStruct((keys, 2 * width), kinds[0])]
        + [jax.ShapeDtypeStruct((width, rows), kinds[1])] * count,
        in_specs=[WHOLE] * (1 + 6 * count + len(given)),
        out_specs=[WHOLE] * (count + 1),
        name="backward",
        **params(24, count * 32 * rows * keys * width, count * 2 * rows * keys),
    )(kv, *stored, *tops, *qs, *grads, *lses, *deltas, *given)
    return out[0], list(out[1:])


def split_rows(value):
    high = value.astype(BF16).astype(F32)
    return [high, value - high]


def collect_kernel(dq, dq_part, own, other, out_part, xhat, weight, gain, bias, *refs):
    parts = refs[:3]
    grad, kept, sib, pair, diag, wide = refs[3:]
    width = dq.shape[0]
    total = own[...] + other[...]
    for part in parts:
        total = total + part[...].astype(F32)
    query = dq[...] + dq_part[...].astype(F32)
    query = jnp.transpose(query * (1.0 / math.sqrt(width)), (1, 0))
    packed = jnp.concatenate([query, total], 1).astype(BF16)
    wide[...] = packed
    for target in (kept, sib, pair, diag):
        target[:256, 3 * width :] = jnp.zeros((256, 256 - 3 * width), BF16)
    regroup(wide, kept, sib, pair, diag)
    moment = dot(packed, xhat[...], TN)
    flipped = jnp.transpose(packed.astype(F32), (1, 0))
    sums = jnp.sum(flipped, axis=1, keepdims=True)
    grad[: 3 * width, :] = (moment * gain[...] + sums * bias[...]).astype(BF16)
    grad[3 * width :, :] = out_part[...]
    held = weight[...].astype(F32)
    rows = split_rows(jnp.sum(held * moment, axis=0, keepdims=True))
    rows += split_rows(jnp.sum(held * sums, axis=0, keepdims=True))
    coded = [row[:, n * 256 : (n + 1) * 256] for row in rows for n in range(4)]
    coded = jnp.concatenate(coded, 0).astype(BF16)
    for target in (kept, sib, pair, diag):
        target[256:, :] = coded


def collect(dq, dq_part, own, other, out_part, xhat, weight, gain, bias, parts):
    width, rows = dq.shape
    quarter = jax.ShapeDtypeStruct((rows // 4 + 16, 256), BF16)
    return pl.pallas_call(
        collect_kernel,
        out_shape=(jax.ShapeDtypeStruct((4 * width, weight.shape[1]), BF16),) + (quarter,) * 4,
        in_specs=[WHOLE] * 12,
        out_specs=(WHOLE,) * 5,
        scratch_shapes=[pltpu.VMEM((rows, 3 * width), BF16)],
        name="collect",
        **params(16, 8 * weight.size * rows, 24 * rows * width),
    )(dq, dq_part, own, other, out_part, xhat, weight, gain, bias, *parts)


def spread_kernel(*refs):
    pieces, weights, outs, held, sems = refs[:4], refs[4:8], refs[8:13], refs[13], refs[14]
    depth = weights[0].shape[0]
    copies = [pltpu.make_async_copy(weights[n], held.at[n], sems.at[n]) for n in range(4)]
    for copy in copies:
        copy.start()
    total = 0
    coded = 0
    for n, piece in enumerate(pieces):
        copies[n].wait()
        total += dot(piece[:256, :depth], held[n])
        coded += piece[256:, :].astype(F32)
    vectors = []
    for v in range(2):
        row = coded[8 * v : 8 * v + 4] + coded[8 * v + 4 : 8 * v + 8]
        vectors.append(jnp.concatenate([row[n : n + 1] for n in range(4)], 1))
    rows = split_rows(vectors[0]) + split_rows(vectors[1])
    rows = jnp.concatenate(rows + [jnp.zeros((12, rows[0].shape[1]), F32)], 0)
    for r in range(4):
        outs[r][...] = total[r * 64 : (r + 1) * 64].astype(outs[r].dtype)
    outs[4][...] = rows.astype(BF16)


def spread(pieces, weights):
    model = weights[0].shape[1]
    return pl.pallas_call(
        spread_kernel,
        out_shape=[jax.ShapeDtypeStruct((64, model), F32 if r == 0 else BF16) for r in range(4)]
        + [jax.ShapeDtypeStruct((16, model), BF16)],
        in_specs=[WHOLE] * 4 + [ANY] * 4,
        out_specs=[WHOLE] * 5,
        scratch_shapes=[
            pltpu.VMEM((4,) + weights[0].shape, BF16),
            pltpu.SemaphoreType.DMA((4,)),
        ],
        name="spread",
        **params(16, 8 * 256 * 768 * 1024, 2 * 4 * weights[0].size),
    )(*pieces, *weights)


def finish_kernel(tokens, cot, gain, own, one, two, three, out):
    normed_grad = own[...] + one[...].astype(F32) + two[...].astype(F32) + three[...].astype(F32)
    xhat, inverse = normalise(tokens[...])
    scaled = normed_grad * gain[...]
    simple = jnp.mean(scaled, axis=-1, keepdims=True)
    product = jnp.mean(scaled * xhat, axis=-1, keepdims=True)
    grad = cot[...].astype(F32) + inverse * (scaled - simple - xhat * product)
    out[...] = grad.astype(BF16)


def finish(tokens, cot, gain, parts):
    return pl.pallas_call(
        finish_kernel,
        out_shape=jax.ShapeDtypeStruct(tokens.shape, BF16),
        in_specs=[WHOLE] * 7,
        out_specs=WHOLE,
        name="finish",
        **params(16, 20 * tokens.size, 12 * tokens.size),
    )(tokens, cot, gain, *parts)


def add_kernel(factor, got, bias_sum, *refs):
    coded, out = refs[:-1], refs[-1]
    total = got[0].astype(F32)
    for n in range(1, got.shape[0]):
        total += got[n].astype(F32)
    height = total.shape[0]
    part = (total * factor).astype(BF16)
    rows = coded[0][...].astype(F32)
    for ref in coded[1:]:
        rows += ref[...].astype(F32)
    vectors = split_rows(rows[0:1] + rows[1:2]) + split_rows(rows[2:3] + rows[3:4])
    vectors += split_rows(bias_sum[...])
    vectors = jnp.concatenate(vectors + [jnp.zeros((2, total.shape[1]), F32)], 0)
    vectors = vectors.astype(BF16)
    for n in range(out.shape[0]):
        out[n, :height, :] = part
        out[n, height:, :] = vectors


def add(got, bias_sum, coded, factor):
    ways, height, model = got.shape
    return pl.pallas_call(
        functools.partial(add_kernel, factor),
        out_shape=jax.ShapeDtypeStruct((ways, height + 8, model), BF16),
        in_specs=[WHOLE] * (2 + len(coded)),
        out_specs=WHOLE,
        name="add",
        **params(16, got.size, 2 * got.size),
    )(got, bias_sum, *coded)


def unpack_kernel(factor, every, qkv, out, bias, gain, shift):
    ways = every.shape[0]
    height = 4 * out.shape[0] // ways
    each = ways // 4
    total = 0
    for n in range(ways):
        rows = every[n, :height, :].astype(F32)
        here = pl.ds((n % each) * height, height)
        if n // each < 3:
            qkv[n // each, here, :] = rows
        else:
            out[here, :] = rows
        total += every[n, height:, :].astype(F32)
    total *= factor
    gain[...] = total[0:1] + total[1:2]
    shift[...] = total[2:3] + total[3:4]
    bias[...] = total[4:5] + total[5:6]


def unpack(every, width, factor):
    model = every.shape[2]
    vector = jax.ShapeDtypeStruct((1, model), F32)
    return pl.pallas_call(
        functools.partial(unpack_kernel, factor),
        out_shape=(
            jax.ShapeDtypeStruct((3, width, model), F32),
            jax.ShapeDtypeStruct((width, model), F32),
            vector,
            vector,
            vector,
        ),
        in_specs=[WHOLE],
        out_specs=(WHOLE,) * 5,
        name="unpack",
        **params(8, every.size, 6 * every.size),
    )(every)


def tie(value, *others):
    return lax.optimization_barrier((value,) + others)[0]


def on_device(
    tokens, cotangent, qkv_weight, out_weight, out_bias, norm_gain_vector, norm_bias_vector
):
    own_tokens = tokens[0]
    own_cot = cotangent[0]
    own_rows, model = own_tokens.shape
    width = qkv_weight.shape[1]
    weight = qkv_weight.reshape(3 * width, model)
    gain = norm_gain_vector[None]
    bias = norm_bias_vector[None]
    rows = HEADS * own_rows

    pieces, table = [own_tokens, to_sibling(own_tokens)], [(0, 0, 0), (0, 1, 0)]
    right = left = own_tokens
    for steps in (1, 2, 3):
        right, left = along_z(right, 1), along_z(left, -1)
        pieces += [right, left, to_sibling(right), to_sibling(left)]
        table += [(-steps, 0, 0), (steps, 0, 0), (-steps, 1, 0), (steps, 1, 0)]
        if steps == 2:
            early = project(table, pieces, weight, gain, bias, width, rows, None)
            pieces, table = [], []
    half = own_rows // 2
    right, left, early = lax.optimization_barrier((right, left, early))
    right, left = along_z(right[:half], 1), along_z(left[half:], -1)
    pieces += [right, left, to_sibling(right), to_sibling(left)]
    table += [(4, 0, 0), (4, 0, half), (4, 1, 0), (4, 1, half)]
    xhat, _, own_kv, queries = project(
        table, pieces, weight, gain, bias, width, rows, early
    )
    cot_all = lax.all_gather(own_cot, "head", axis=0, tiled=True)

    other_q = to_half(queries)
    arrived = [along_x(own_kv, steps) for steps in OFFSETS]
    held_kv, cot_all, _ = lax.optimization_barrier((own_kv, cot_all, other_q))
    out_full = lax.all_gather(tie(out_weight, cot_all), "head", axis=0, tiled=True)
    grads, bias_sum = grad_att(cot_all, out_weight)
    other_grads = to_half(grads)
    qs = (queries, other_q)
    states, stored, tops = [None, None], [[], []], [[], []]
    for wave in ([held_kv], arrived[:2], arrived[2:]):
        for n in range(2):
            states[n], probs, top = forward(wave, qs[n], states[n])
            stored[n] += probs
            tops[n] += top
    got = to_half(message(*states))
    later_weight = tie(weight, stored[0][1])
    w_pair, w_sib = to_pair(later_weight), to_sibling(later_weight)
    w_diag = to_sibling(w_pair)
    got, w_pair, w_sib, w_diag = lax.optimization_barrier((got, w_pair, w_sib, w_diag))
    gs = (grads, other_grads)
    att_t, lses, deltas, quarters = middle(*states, got, gs)

    quarters = [
        quarters[0],
        to_sibling(quarters[1]),
        to_pair(quarters[2]),
        to_diagonal(quarters[3]),
    ]

    dqs = None
    home = []
    for count, n in enumerate((2, 0, 1)):
        part, dqs = backward(
            arrived[n],
            [stored[0][n + 1], stored[1][n + 1]],
            [tops[0][n + 1], tops[1][n + 1]],
            qs,
            gs,
            lses,
            deltas,
            dqs,
            (BF16, F32),
        )
        home.append(along_x(part, -OFFSETS[n]))
        if count == 0:
            quarters, *dqs = lax.optimization_barrier((quarters, *dqs))
            att_pieces = lay(quarters)
            att_pieces = [att_pieces[0]] + [along_z(att_pieces[r], 2 * r) for r in (1, 2, 3)]
        if count == 2:
            home[0], att_pieces, *dqs = lax.optimization_barrier((home[0], att_pieces, *dqs))
    own_parts = []
    for n in (1, 0):
        part, (dqs[n],) = backward(
            held_kv,
            [stored[n][0]],
            [tops[n][0]],
            [qs[n]],
            [gs[n]],
            [lses[n]],
            [deltas[n]],
            [dqs[n]],
            (F32, F32 if n == 0 else BF16),
        )
        own_parts.append(part)
    dq_part = to_half(dqs[1])
    out_part = dot(att_t, cot_all).astype(BF16)

    matrix, kept, sib, pair, diag = collect(
        dqs[0], dq_part, own_parts[1], own_parts[0], out_part, xhat, weight, gain, bias, home
    )
    sib, pair, diag = to_sibling(sib), to_pair(pair), to_diagonal(diag)
    scattered = spread((kept, sib, pair, diag), (weight, w_sib, w_pair, w_diag))
    coded = [scattered[4]] + [along_z(scattered[4], 2 * r) for r in (1, 2, 3)]
    parts = [scattered[0]] + [along_z(scattered[r], 2 * r) for r in (1, 2, 3)]

    ways = lax.axis_size("dp") * lax.axis_size("blk")
    factor = 1.0 / math.sqrt(ways * rows)
    matrix = tie(matrix, sib).reshape(ways, 4 * width // ways, model)
    got = lax.all_to_all(matrix, ("dp", "blk"), 0, 0, tiled=True)
    back = add(got, bias_sum, coded, factor)
    out_full, back = lax.optimization_barrier((out_full, back))
    every = lax.all_to_all(back, ("dp", "blk"), 0, 0, tiled=True)
    layer_rows = layer(own_tokens, out_bias[None], out_full, att_pieces)
    grad_rows = finish(own_tokens, own_cot, gain, parts)
    qkv_grad, out_grad, bias_grad, gain_grad, shift_grad = unpack(every, width, factor)
    return (
        layer_rows[None],
        grad_rows[None],
        qkv_grad,
        out_grad,
        bias_grad[0],
        gain_grad[0],
        shift_grad[0],
    )


def solution(mesh):
    tokens = P("dp", ("head", "blk"), None)
    heads = P("head", None)
    return jax.shard_map(
        on_device,
        mesh=mesh,
        in_specs=(tokens, tokens, P(None, "head", None), heads, P(), P(), P()),
        out_specs=(tokens, tokens, P(None, "head", None), heads, P(), P(), P()),
        check_vma=False,
    )
```

```python
import functools
import math

import jax
import jax.numpy as jnp
from jax import lax
from jax.experimental import pallas as pl
from jax.experimental.pallas import tpu as pltpu
from jax.sharding import PartitionSpec as P

HEADS = 16
EPSILON = 1e-06
ZN = 8
XN = 4
F32 = jnp.float32
BF16 = jnp.bfloat16
WHOLE = pl.BlockSpec(memory_space=pltpu.VMEM)
ANY = pl.BlockSpec(memory_space=pl.ANY)
NT = (((1,), (1,)), ((), ()))
TN = (((0,), (0,)), ((), ()))
NN = (((1,), (0,)), ((), ()))

OFFSETS = (1, 3, 2)


def dot(a, b, dims=NN):
    return lax.dot_general(a, b, dims, preferred_element_type=F32)


def params(mib, flops=0, moved=0, trans=0):
    return dict(
        compiler_params=pltpu.CompilerParams(vmem_limit_bytes=mib * 2**20),
        cost_estimate=pl.CostEstimate(flops=flops, bytes_accessed=moved, transcendentals=trans),
    )


def permute(value, axis, count, target):
    return lax.ppermute(value, axis, [(i, target(i)) for i in range(count)])


def along_z(value, steps):
    return permute(value, "head", HEADS, lambda h: ((h // 2 + steps) % ZN) * 2 + h % 2)


def to_sibling(value):
    return permute(value, "head", HEADS, lambda h: h ^ 1)


def to_pair(value):
    return permute(value, "head", HEADS, lambda h: h ^ 2)


def to_diagonal(value):
    return permute(value, "head", HEADS, lambda h: h ^ 3)


def along_x(value, steps):
    return permute(value, "blk", 2 * XN, lambda b: (b // XN) * XN + (b % XN + steps) % XN)


def to_half(value):
    return permute(value, "blk", 2 * XN, lambda b: b ^ XN)


def fetch(sources, held, sems):
    copies = [pltpu.make_async_copy(a, b, sems.at[n]) for n, (a, b) in enumerate(zip(sources, held))]
    for copy in copies:
        copy.start()

    def ready(n):
        copies[n].wait()
        return held[n]

    return ready


def room(values):
    return [pltpu.VMEM(v.shape, v.dtype) for v in values] + [
        pltpu.SemaphoreType.DMA((len(values),))
    ]


def position():
    head = lax.axis_index("head")
    return head // 2, lax.rem(head, 2)


def normalise(rows):
    values = rows.astype(F32)
    shifted = values - jnp.mean(values, axis=-1, keepdims=True)
    spread = jnp.mean(shifted * shifted, axis=-1, keepdims=True)
    inverse = lax.rsqrt(spread + EPSILON)
    return shifted * inverse, inverse


def project_kernel(table, chained, *refs):
    count = len(table)
    pieces = refs[:count]
    weight, gain, bias = refs[count : count + 3]
    refs = refs[count + 3 + (4 if chained else 0) :]
    xhat_out, cot_out, qg_out, kv_out, normed, cots = refs
    z, core = position()
    width = weight.shape[0] // 4
    own_rows = 64
    places, grads = [], []
    for piece, (steps, flip, kind) in zip(pieces, table):
        own = core if flip == 0 else 1 - core
        start = lax.rem(z + steps + ZN, ZN) * 2 * own_rows + own * own_rows
        there = pl.ds(pl.multiple_of(start, own_rows), own_rows)
        if kind != "cot":
            first = len(places) * own_rows
            xhat, _ = normalise(piece[:own_rows, :])
            xhat_out[there, :] = xhat.astype(BF16)
            normed[pl.ds(first, own_rows), :] = (xhat * gain[...] + bias[...]).astype(BF16)
            places.append((there, first, first + own_rows))
        if kind != "tok":
            first = len(grads) * own_rows
            rows = piece[piece.shape[0] - own_rows :, :]
            cot_out[there, :] = rows
            cots[pl.ds(first, own_rows), :] = rows
            grads.append((there, first, first + own_rows))
    packed = dot(normed[...], weight[: 3 * width, :], NT)
    queries = packed[:, :width].astype(BF16).astype(F32) * (1.0 / math.sqrt(width))
    queries = queries.astype(BF16)
    pairs = packed[:, width:].astype(BF16)
    for there, first, last in places:
        qg_out[there, :width] = queries[first:last]
        kv_out[there, :] = pairs[first:last]
    back = dot(cots[...], weight[3 * width :, :], NT).astype(BF16)
    for there, first, last in grads:
        qg_out[there, width:] = back[first:last]


def project(table, pieces, weight, gain, bias, rows, before):
    total = sum(64 for entry in table if entry[2] != "cot")
    width, model = weight.shape[0] // 4, weight.shape[1]
    chained = [] if before is None else list(before)
    first = 3 + len(pieces)
    return pl.pallas_call(
        functools.partial(project_kernel, table, before is not None),
        out_shape=(
            jax.ShapeDtypeStruct((rows, model), BF16),
            jax.ShapeDtypeStruct((rows, model), BF16),
            jax.ShapeDtypeStruct((rows, 2 * width), BF16),
            jax.ShapeDtypeStruct((rows, 2 * width), BF16),
        ),
        in_specs=[WHOLE] * (len(pieces) + 3 + len(chained)),
        out_specs=(WHOLE,) * 4,
        scratch_shapes=[pltpu.VMEM((total, model), BF16)] * 2,
        input_output_aliases={first + n: n for n in range(len(chained))},
        name="project",
        **params(16, 2 * total * model * 4 * width, 4 * total * model * 2),
    )(*pieces, weight, gain, bias, *chained)


def order_kernel(*refs):
    count = len(refs) // 4
    swap = lax.axis_index("blk") >= XN
    for n in range(count):
        own, other = refs[n][...], refs[count + n][...]
        refs[2 * count + n][...] = jnp.where(swap, other, own)
        refs[3 * count + n][...] = jnp.where(swap, own, other)


def order(own, other):
    count = len(own)
    out = pl.pallas_call(
        order_kernel,
        out_shape=[jax.ShapeDtypeStruct(v.shape, v.dtype) for v in own] * 2,
        in_specs=[WHOLE] * (2 * count),
        out_specs=[WHOLE] * (2 * count),
        name="order",
        **params(8, own[0].size, 8 * own[0].size),
    )(*own, *other)
    return out[:count], out[count:]


def forward_kernel(count, first, *refs):
    blocks = refs[:count]
    q_ref = refs[count]
    rest = refs[count + 1 :]
    if first:
        top = total = part = None
    else:
        top, total, part = rest[0][...], rest[1][...], rest[2][...]
        rest = rest[3:]
    m_out, l_out, acc_out = rest[:3]
    p_out, step_out = rest[3 : 3 + count], rest[3 + count : 3 + 2 * count]
    width = q_ref.shape[1] // 2
    queries = q_ref[:, :width]
    for n in range(count):
        kv = blocks[n]
        scores = dot(kv[:, :width], queries, NT)
        new = jnp.max(scores, axis=0, keepdims=True)
        if top is not None:
            new = jnp.maximum(top, new)
        probs = jnp.exp(scores - new)
        weights = probs.astype(BF16)
        p_out[n][...] = weights
        step_out[n][...] = new
        sums = jnp.sum(probs, axis=0, keepdims=True)
        values = dot(kv[:, width:], weights, TN)
        if top is None:
            total, part = sums, values
        else:
            shrink = jnp.exp(top - new)
            total, part = total * shrink + sums, part * shrink + values
        top = new
    m_out[...], l_out[...], acc_out[...] = top, total, part


def forward(blocks, queries, state):
    count = len(blocks)
    rows, width = queries.shape[0], queries.shape[1] // 2
    keys = blocks[0].shape[0]
    first = state is None
    states = [(1, rows), (1, rows), (width, rows)]
    out = pl.pallas_call(
        functools.partial(forward_kernel, count, first),
        out_shape=[jax.ShapeDtypeStruct(s, F32) for s in states]
        + [jax.ShapeDtypeStruct((keys, rows), BF16)] * count
        + [jax.ShapeDtypeStruct((1, rows), F32)] * count,
        in_specs=[WHOLE] * (count + 1 + (0 if first else 3)),
        out_specs=[WHOLE] * (3 + 2 * count),
        name="forward",
        **params(
            24,
            count * 16 * rows * keys * width, count * 2 * rows * keys, count * rows * keys
        ),
    )(*blocks, queries, *([] if first else state))
    return out[:3], out[3 : 3 + count], out[3 + count :]


def split_thrice(value):
    high = value.astype(BF16).astype(F32)
    rest = value - high
    middle_part = rest.astype(BF16).astype(F32)
    return [high, middle_part, rest - middle_part]


def message_kernel(top, total, part, out):
    width, rows = part.shape
    out[:width, :] = part[...].astype(BF16)
    coded = split_thrice(top[...]) + split_thrice(total[...])
    coded = jnp.concatenate(coded + [jnp.zeros((10, rows), F32)], 0)
    out[width:, :] = coded.astype(BF16)


def message(top, total, part):
    width, rows = part.shape
    return pl.pallas_call(
        message_kernel,
        out_shape=jax.ShapeDtypeStruct((width + 16, rows), BF16),
        in_specs=[WHOLE] * 3,
        out_specs=WHOLE,
        name="message",
        **params(8, 4 * rows * width, 6 * rows * width),
    )(top, total, part)


def middle_kernel(top, total, part, got, qg, *refs):
    width = part.shape[0]
    earlier = refs[0] if len(refs) == 5 else None
    att_t, lse, delta = refs[1:4] if earlier is not None else refs
    coded = got[width:, :].astype(F32)
    their_top = coded[0:1] + coded[1:2] + coded[2:3]
    their_total = coded[3:4] + coded[4:5] + coded[5:6]
    new = jnp.maximum(top[...], their_top)
    mine, theirs = jnp.exp(top[...] - new), jnp.exp(their_top - new)
    both = total[...] * mine + their_total * theirs
    summed = part[...] * mine + got[:width, :].astype(F32) * theirs
    lse[...] = new + jnp.log(both)
    attended = (summed / both).astype(BF16)
    wide = attended.astype(F32)
    back = jnp.transpose(qg[:, width:].astype(F32), (1, 0))
    delta[...] = jnp.sum(back * wide, axis=0, keepdims=True)
    if earlier is not None:
        wide = jnp.where(lax.axis_index("blk") >= XN, wide, earlier[...].astype(F32))
        refs[-1][...] = jnp.transpose(wide, (1, 0)).astype(BF16)
    att_t[...] = wide.astype(BF16)


def regroup(rows, kept, sib, pair, diag):
    z, core = position()
    group, parity = z // 2, lax.rem(z, 2)
    width = rows.shape[1]
    for r in range(ZN // 2):
        base = lax.rem(group + r, ZN // 2) * 256
        to = pl.ds(r * 64, 64)
        for target, dp, dc in ((kept, 0, 0), (sib, 0, 1), (pair, 1, 0), (diag, 1, 1)):
            p = parity if dp == 0 else 1 - parity
            c = core if dc == 0 else 1 - core
            at = pl.multiple_of(base + p * 128 + c * 64, 64)
            target[to, :width] = rows[pl.ds(at, 64), :]


def middle(state, got, qg, earlier):
    width, rows = state[2].shape
    row = jax.ShapeDtypeStruct((1, rows), F32)
    last = earlier is not None
    att = (jax.ShapeDtypeStruct((rows, width), BF16),) if last else ()
    return pl.pallas_call(
        middle_kernel,
        out_shape=(jax.ShapeDtypeStruct((width, rows), BF16), row, row) + att,
        in_specs=[WHOLE] * (6 if last else 5),
        out_specs=(WHOLE,) * (4 if last else 3),
        name="middle",
        **params(16, 10 * rows * width, 8 * rows * width),
    )(*state, got, qg, *([earlier] if last else []))


def backward_kernel(own, has_dq, has_dkv, kv, *refs):
    count = 1 if own is None else 2
    stored, top = refs[:2]
    qgs, lses, deltas = (refs[2 + n * count : 2 + (n + 1) * count] for n in range(3))
    rest = refs[2 + 3 * count :]
    dq_in = rest[:count] if has_dq else None
    rest = rest[count:] if has_dq else rest
    dkv_in = rest[0] if has_dkv else None
    out, dq_out = rest[-2:]

    def pick(pair, *at):
        if own is None:
            return pair[0][at]
        swap = lax.axis_index("blk") >= XN
        first, second = pair if own else (pair[1], pair[0])
        return jnp.where(swap, second[at], first[at])

    width = kv.shape[1] // 2
    tile = 512
    dk = dkv_in[:, :width] if has_dkv else 0
    dv = dkv_in[:, width:] if has_dkv else 0
    for t in range(kv.shape[0] // tile):
        here = pl.ds(t * tile, tile)
        every = slice(None)
        qg = pick(qgs, here, every)
        q, grad = qg[:, :width], qg[:, width:]
        factor = jnp.exp(top[:, here] - pick(lses, every, here))
        prob_grad = dot(kv[:, width:], grad, NT)
        probs = stored[:, here].astype(F32) * factor
        score_grad = (probs * (prob_grad - pick(deltas, every, here))).astype(BF16)
        dv += dot(probs.astype(BF16), grad)
        dk += dot(score_grad, q)
        dq = dot(kv[:, :width], score_grad, TN)
        if has_dq:
            dq += pick(dq_in, every, here)
        dq_out[:, here] = dq.astype(dq_out.dtype)
    out[:, :width] = dk.astype(out.dtype)
    out[:, width:] = dv.astype(out.dtype)


def backward(own, kv, stored, top, qgs, lses, deltas, dqs, dkv, kinds):
    rows, width = qgs[0].shape[0], qgs[0].shape[1] // 2
    keys = kv.shape[0]
    given = ([] if dqs is None else list(dqs)) + ([] if dkv is None else [dkv])
    operands = [kv, stored, top, *qgs, *lses, *deltas, *given]
    return pl.pallas_call(
        functools.partial(backward_kernel, own, dqs is not None, dkv is not None),
        out_shape=[
            jax.ShapeDtypeStruct((keys, 2 * width), kinds[0]),
            jax.ShapeDtypeStruct((width, rows), kinds[1]),
        ],
        in_specs=[WHOLE] * len(operands),
        out_specs=[WHOLE] * 2,
        name="backward",
        **params(24, 32 * rows * keys * width, 2 * rows * keys),
    )(*operands)


def out_kernel(att_t, cot, part, sums):
    part[...] = dot(att_t[...], cot[...]).astype(BF16)
    sums[...] = jnp.sum(cot[...].astype(F32), axis=0, keepdims=True)


def out_sums(att_t, cot):
    return pl.pallas_call(
        out_kernel,
        out_shape=(
            jax.ShapeDtypeStruct((att_t.shape[0], cot.shape[1]), BF16),
            jax.ShapeDtypeStruct((1, cot.shape[1]), F32),
        ),
        in_specs=[WHOLE] * 2,
        out_specs=(WHOLE,) * 2,
        name="out_sums",
        **params(16, 2 * att_t.size * cot.shape[1], 2 * cot.size),
    )(att_t, cot)


def split_rows(value):
    high = value.astype(BF16).astype(F32)
    return [high, value - high]


def collect_kernel(dq, dq_part, own, att, out_part, xhat, weight, gain, bias, *refs):
    parts = refs[:3]
    grad, kept, sib, far, wide = refs[3:]
    height = kept.shape[0]
    pair, diag = far.at[pl.ds(0, height), :], far.at[pl.ds(height, height), :]
    width = dq.shape[0]
    total = own[...]
    for part in parts:
        total = total + part[...].astype(F32)
    query = dq[...] + dq_part[...].astype(F32)
    query = jnp.transpose(query * (1.0 / math.sqrt(width)), (1, 0))
    packed = jnp.concatenate([query, total], 1).astype(BF16)
    wide[:, : 3 * width] = packed
    wide[:, 3 * width :] = att[...]
    regroup(wide, kept, sib, pair, diag)
    moment = dot(packed, xhat[...], TN)
    flipped = jnp.transpose(packed.astype(F32), (1, 0))
    sums = jnp.sum(flipped, axis=1, keepdims=True)
    grad[: 3 * width, :] = (moment * gain[...] + sums * bias[...]).astype(BF16)
    grad[3 * width :, :] = out_part[...]
    held = weight[: 3 * width, :].astype(F32)
    rows = split_rows(jnp.sum(held * moment, axis=0, keepdims=True))
    rows += split_rows(jnp.sum(held * sums, axis=0, keepdims=True))
    coded = [row[:, n * 256 : (n + 1) * 256] for row in rows for n in range(4)]
    coded = jnp.concatenate(coded, 0).astype(BF16)
    for target in (kept, sib, pair, diag):
        target[256:, :] = coded


def collect(dq, dq_part, own, att, out_part, xhat, weight, gain, bias, parts):
    width, rows = dq.shape
    quarter = jax.ShapeDtypeStruct((rows // 4 + 16, 256), BF16)
    double = jax.ShapeDtypeStruct((2 * (rows // 4 + 16), 256), BF16)
    return pl.pallas_call(
        collect_kernel,
        out_shape=(jax.ShapeDtypeStruct(weight.shape, BF16), quarter, quarter, double),
        in_specs=[WHOLE] * 12,
        out_specs=(WHOLE,) * 4,
        scratch_shapes=[pltpu.VMEM((rows, 4 * width), BF16)],
        name="collect",
        **params(16, 8 * weight.size * rows, 24 * rows * width),
    )(dq, dq_part, own, att, out_part, xhat, weight, gain, bias, *parts)


def spread_kernel(*refs):
    own, own_laid, vectors_out, up, down, near_up, near_laid_up, near_down, near_laid_down = refs[8:17]
    held, sems = refs[17:25], refs[25]
    height = refs[0].shape[0]
    sources = [refs[0], refs[1], refs[2].at[pl.ds(0, height), :], refs[3].at[pl.ds(height, height), :]]
    ready = fetch([*sources, *refs[4:8]], held, sems)
    depth = 3 * refs[4].shape[0] // 4
    total = laid = coded = 0
    for n in range(4):
        piece, weight = ready(n), ready(4 + n)
        total += dot(piece[:256, :depth], weight[:depth, :])
        laid += dot(piece[:256, depth:], weight[depth:, :])
        coded += piece[256:, :].astype(F32)
    vectors = []
    for v in range(2):
        row = coded[8 * v : 8 * v + 4] + coded[8 * v + 4 : 8 * v + 8]
        vectors.append(jnp.concatenate([row[n : n + 1] for n in range(4)], 1))
    rows = split_rows(vectors[0]) + split_rows(vectors[1])
    rows = jnp.concatenate(rows + [jnp.zeros((4, rows[0].shape[1]), F32)], 0).astype(BF16)
    own[...], own_laid[...] = total[:64], laid[:64]
    vectors_out[...] = rows
    up[:64, :], down[:64, :] = total[128:192].astype(BF16), laid[128:192].astype(BF16)
    up[64:, :], down[64:, :] = rows, rows
    near_up[...], near_laid_up[...] = total[64:128], laid[64:128].astype(BF16)
    near_down[...], near_laid_down[...] = total[192:].astype(BF16), laid[192:]


def spread(pieces, weights):
    model = weights[0].shape[1]
    shape = lambda rows, kind: jax.ShapeDtypeStruct((rows, model), kind)
    height = pieces[0].shape
    held = [jax.ShapeDtypeStruct(height, BF16)] * 4
    return pl.pallas_call(
        spread_kernel,
        out_shape=[
            shape(64, F32),
            shape(64, F32),
            shape(8, BF16),
            shape(72, BF16),
            shape(72, BF16),
            shape(64, F32),
            shape(64, BF16),
            shape(64, BF16),
            shape(64, F32),
        ],
        in_specs=[ANY] * 8,
        out_specs=[WHOLE] * 9,
        scratch_shapes=room([*held, *weights]),
        name="spread",
        **params(24, 8 * 256 * 768 * 1024, 2 * 4 * weights[0].size),
    )(*pieces, *weights)


def relay_kernel(got_up, got_down, near_up, near_laid_up, near_down, near_laid_down, up, down):
    up[:64, :] = (near_up[...] + got_up[:64, :].astype(F32)).astype(BF16)
    up[64:, :] = near_laid_up[...]
    down[:64, :] = near_down[...]
    down[64:, :] = (near_laid_down[...] + got_down[:64, :].astype(F32)).astype(BF16)


def relay(got_up, got_down, near):
    model = got_up.shape[1]
    return pl.pallas_call(
        relay_kernel,
        out_shape=[jax.ShapeDtypeStruct((128, model), BF16)] * 2,
        in_specs=[WHOLE] * 6,
        out_specs=[WHOLE] * 2,
        name="relay",
        **params(8, got_up.size, 8 * got_up.size),
    )(got_up, got_down, *near)


def finish_kernel(tokens, cot, gain, out_bias, own, own_laid, up, down, grad_out, layer_out):
    normed_grad = own[...] + up[:64, :].astype(F32) + down[:64, :].astype(F32)
    xhat, inverse = normalise(tokens[...])
    scaled = normed_grad * gain[...]
    simple = jnp.mean(scaled, axis=-1, keepdims=True)
    product = jnp.mean(scaled * xhat, axis=-1, keepdims=True)
    grad = cot[...].astype(F32) + inverse * (scaled - simple - xhat * product)
    grad_out[...] = grad.astype(BF16)
    laid = own_laid[...] + up[64:, :].astype(F32) + down[64:, :].astype(F32)
    layer_out[...] = (tokens[...].astype(F32) + laid + out_bias[...]).astype(BF16)


def finish(tokens, cot, gain, out_bias, own, own_laid, up, down):
    return pl.pallas_call(
        finish_kernel,
        out_shape=[jax.ShapeDtypeStruct(tokens.shape, BF16)] * 2,
        in_specs=[WHOLE] * 8,
        out_specs=[WHOLE] * 2,
        name="finish",
        **params(16, 20 * tokens.size, 12 * tokens.size),
    )(tokens, cot, gain, out_bias, own, own_laid, up, down)


def add_kernel(factor, got, bias_sum, *refs):
    coded, out = refs[:4], refs[4]
    total = got[0].astype(F32)
    for n in range(1, got.shape[0]):
        total += got[n].astype(F32)
    height = total.shape[0]
    part = (total * factor).astype(BF16)
    rows = 0
    for ref in coded:
        rows += ref[ref.shape[0] - 8 :, :].astype(F32)
    vectors = split_rows(rows[0:1] + rows[1:2]) + split_rows(rows[2:3] + rows[3:4])
    vectors += split_rows(bias_sum[...])
    vectors = jnp.concatenate(vectors + [jnp.zeros((2, total.shape[1]), F32)], 0)
    vectors = vectors.astype(BF16)
    for n in range(out.shape[0]):
        out[n, :height, :] = part
        out[n, height:, :] = vectors


def add(got, bias_sum, coded, factor):
    ways, height, model = got.shape
    return pl.pallas_call(
        functools.partial(add_kernel, factor),
        out_shape=jax.ShapeDtypeStruct((ways, height + 8, model), BF16),
        in_specs=[WHOLE] * 6,
        out_specs=WHOLE,
        name="add",
        **params(16, got.size, 2 * got.size),
    )(got, bias_sum, *coded)


def unpack_kernel(factor, every, qkv, out, bias, gain, shift):
    ways = every.shape[0]
    height = 4 * out.shape[0] // ways
    each = ways // 4
    total = 0
    for n in range(ways):
        rows = every[n, :height, :].astype(F32)
        here = pl.ds((n % each) * height, height)
        if n // each < 3:
            qkv[n // each, here, :] = rows
        else:
            out[here, :] = rows
        total += every[n, height:, :].astype(F32)
    total *= factor
    gain[...] = total[0:1] + total[1:2]
    shift[...] = total[2:3] + total[3:4]
    bias[...] = total[4:5] + total[5:6]


def unpack(every, width, factor):
    model = every.shape[2]
    vector = jax.ShapeDtypeStruct((1, model), F32)
    return pl.pallas_call(
        functools.partial(unpack_kernel, factor),
        out_shape=(
            jax.ShapeDtypeStruct((3, width, model), F32),
            jax.ShapeDtypeStruct((width, model), F32),
            vector,
            vector,
            vector,
        ),
        in_specs=[WHOLE],
        out_specs=(WHOLE,) * 5,
        name="unpack",
        **params(8, every.size, 6 * every.size),
    )(every)


def tie(value, *others):
    return lax.optimization_barrier((value,) + others)[0]


def on_device(
    tokens, cotangent, qkv_weight, out_weight, out_bias, norm_gain_vector, norm_bias_vector
):
    own_tokens = tokens[0]
    own_cot = cotangent[0]
    own_rows, model = own_tokens.shape
    width = qkv_weight.shape[1]
    weight = jnp.concatenate([qkv_weight.reshape(3 * width, model), out_weight], 0)
    gain = norm_gain_vector[None]
    bias = norm_bias_vector[None]
    rows = HEADS * own_rows

    both = jnp.concatenate([own_tokens, own_cot], 0)
    pieces, table = [both, to_sibling(both)], [(0, 0, "both"), (0, 1, "both")]
    right = left = both
    early = None
    weights = (weight, gain, bias)
    for steps in (1, 2, 3):
        right, left = along_z(right, 1), along_z(left, -1)
        pieces += [right, left, to_sibling(right), to_sibling(left)]
        table += [(-steps, 0, "both"), (steps, 0, "both"), (-steps, 1, "both"), (steps, 1, "both")]
        if steps == 2:
            early = project(table, pieces, *weights, rows, None)
            pieces, table = [], []
    right, early = lax.optimization_barrier((right, early))
    right = along_z(right, 1)
    pieces += [right, to_sibling(right)]
    table += [(4, 0, "both"), (4, 1, "both")]
    xhat, cot_all, own_qg, own_kv = project(table, pieces, *weights, rows, early)

    other_qg = to_half(own_qg)
    arrived = [along_x(own_kv, steps) for steps in OFFSETS]
    other_qg, arrived[0], arrived[1], held_kv = lax.optimization_barrier(
        (other_qg, arrived[0], arrived[1], own_kv)
    )
    later_weight = tie(weight, held_kv)
    w_pair, w_sib = to_pair(later_weight), to_sibling(later_weight)
    own_state, own_probs, own_top = forward([held_kv], own_qg, None)
    other_state, other_probs, other_top = forward([held_kv], other_qg, None)
    first, second = order([own_qg, *own_state], [other_qg, *other_state])
    qgs = [first[0], second[0]]
    states = [first[1:], second[1:]]
    stored, tops, lses, deltas = [[], []], [[], []], [None, None], [None, None]
    got = [None, None]
    for n, waves in enumerate(((arrived[:2], arrived[2:]), (arrived,))):
        for wave in waves:
            states[n], probs, top = forward(wave, qgs[n], states[n])
            stored[n] += probs
            tops[n] += top
        got[n] = to_half(message(*states[n]))
        if n == 0:
            *states[0], qgs[1], w_pair = lax.optimization_barrier((*states[0], qgs[1], w_pair))
            w_diag = to_sibling(w_pair)
    got[0], w_pair, w_sib, w_diag = lax.optimization_barrier((got[0], w_pair, w_sib, w_diag))

    early_att, lses[0], deltas[0] = middle(states[0], got[0], qgs[0], None)
    dqs = [None, None]
    far = (2, 0, 1)
    parts = {}
    home = []
    for n in range(2):
        if n == 1:
            got[1], dqs[0] = lax.optimization_barrier((got[1], dqs[0]))
            att_t, lses[1], deltas[1], att = middle(states[1], got[1], qgs[1], early_att)
        for k in far:
            parts[k], dqs[n] = backward(
                None,
                arrived[k],
                stored[n][k],
                tops[n][k],
                [qgs[n]],
                [lses[n]],
                [deltas[n]],
                None if dqs[n] is None else [dqs[n]],
                None if n == 0 else parts[k],
                (F32 if n == 0 else BF16, F32),
            )
            if n == 1:
                home.append(along_x(parts[k], -OFFSETS[k]))
    own_part = None
    last = [None, None]
    for own in (False, True):
        own_part, last[own] = backward(
            own,
            own_kv,
            own_probs[0] if own else other_probs[0],
            own_top[0] if own else other_top[0],
            qgs,
            lses,
            deltas,
            dqs,
            own_part,
            (F32, F32 if own else BF16),
        )
        if not own:
            dq_part = to_half(last[0])
            home[0], own_part = lax.optimization_barrier((home[0], own_part))
    out_part, bias_sum = out_sums(tie(att_t, last[1]), cot_all)

    matrix, kept, sib, far = collect(
        last[1], dq_part, own_part, att, out_part, xhat, weight, gain, bias, home
    )
    sib, far = to_sibling(sib), to_pair(far)
    near = to_sibling(far)
    own, own_laid, coded, up, down, *nearest = spread(
        (kept, sib, far, near), (weight, w_sib, w_pair, w_diag)
    )
    got_up, got_down, got_coded = along_z(up, 2), along_z(down, -2), along_z(coded, 4)
    up, down = relay(got_up, got_down, nearest)

    ways = lax.axis_size("dp") * lax.axis_size("blk")
    factor = 1.0 / math.sqrt(ways * rows)
    matrix = tie(matrix, near).reshape(ways, 4 * width // ways, model)
    got = lax.all_to_all(matrix, ("dp", "blk"), 0, 0, tiled=True)
    got, up, down = lax.optimization_barrier((got, up, down))
    back = add(got, bias_sum, (coded, got_up, got_down, got_coded), factor)
    every = lax.all_to_all(back, ("dp", "blk"), 0, 0, tiled=True)
    grad_rows, layer_rows = finish(
        own_tokens, own_cot, gain, out_bias[None], own, own_laid, along_z(up, 2), along_z(down, -2)
    )
    qkv_grad, out_grad, bias_grad, gain_grad, shift_grad = unpack(every, width, factor)
    return (
        layer_rows[None],
        grad_rows[None],
        qkv_grad,
        out_grad,
        bias_grad[0],
        gain_grad[0],
        shift_grad[0],
    )


def solution(mesh):
    tokens = P("dp", ("head", "blk"), None)
    heads = P("head", None)
    return jax.shard_map(
        on_device,
        mesh=mesh,
        in_specs=(tokens, tokens, P(None, "head", None), heads, P(), P(), P()),
        out_specs=(tokens, tokens, P(None, "head", None), heads, P(), P(), P()),
        check_vma=False,
    )
```

```python
import functools
import math

import jax
import jax.numpy as jnp
from jax import lax
from jax.experimental import pallas as pl
from jax.experimental.pallas import tpu as pltpu
from jax.sharding import PartitionSpec as P

HEADS = 16
EPSILON = 1e-06
ZN = 8
XN = 4
F32 = jnp.float32
BF16 = jnp.bfloat16
WHOLE = pl.BlockSpec(memory_space=pltpu.VMEM)
HBM = pl.BlockSpec(memory_space=pltpu.HBM)
NT = (((1,), (1,)), ((), ()))
TN = (((0,), (0,)), ((), ()))
NN = (((1,), (0,)), ((), ()))

OFFSETS = (1, 3, 2)

EARLY = ((0, 0), (0, 1), (-1, 0), (1, 0), (-1, 1), (1, 1), (-2, 0), (2, 0), (-2, 1), (2, 1))
LATE = ((-3, 0), (3, 0), (-3, 1), (3, 1), (4, 0), (4, 1))
OWN_ROWS = 64
PLACE = {(steps % ZN, flip): n * OWN_ROWS for n, (steps, flip) in enumerate(EARLY + LATE)}


def dot(a, b, dims=NN):
    return lax.dot_general(a, b, dims, preferred_element_type=F32)


def params(mib, flops=0, moved=0, trans=0):
    return dict(
        compiler_params=pltpu.CompilerParams(vmem_limit_bytes=mib * 2**20),
        cost_estimate=pl.CostEstimate(flops=flops, bytes_accessed=moved, transcendentals=trans),
    )


def permute(value, axis, count, target):
    return lax.ppermute(value, axis, [(i, target(i)) for i in range(count)])


def along_z(value, steps):
    return permute(value, "head", HEADS, lambda h: ((h // 2 + steps) % ZN) * 2 + h % 2)


def to_sibling(value):
    return permute(value, "head", HEADS, lambda h: h ^ 1)


def to_pair(value):
    return permute(value, "head", HEADS, lambda h: h ^ 2)


def to_diagonal(value):
    return permute(value, "head", HEADS, lambda h: h ^ 3)


def along_x(value, steps):
    return permute(value, "blk", 2 * XN, lambda b: (b // XN) * XN + (b % XN + steps) % XN)


def to_half(value):
    return permute(value, "blk", 2 * XN, lambda b: b ^ XN)


def fetch(sources, held, sems, finish_all=False):
    copies = [pltpu.make_async_copy(a, b, sems.at[n]) for n, (a, b) in enumerate(zip(sources, held))]
    for copy in copies:
        copy.start()

    if finish_all:
        for copy in copies:
            copy.wait()

    def ready(n):
        copies[n].wait()
        return held[n]

    return ready


def room(values):
    return [pltpu.VMEM(v.shape, v.dtype) for v in values] + [
        pltpu.SemaphoreType.DMA((len(values),))
    ]


def position():
    head = lax.axis_index("head")
    return head // 2, lax.rem(head, 2)


def normalise(rows):
    values = rows.astype(F32)
    shifted = values - jnp.mean(values, axis=-1, keepdims=True)
    spread = jnp.mean(shifted * shifted, axis=-1, keepdims=True)
    inverse = lax.rsqrt(spread + EPSILON)
    return shifted * inverse, inverse


def project_kernel(base, count, *refs):
    pieces, others = list(refs[:count]), list(refs[count : 2 * count])
    weight, norm = refs[2 * count : 2 * count + 2]
    gain, bias = norm[0:1, :], norm[1:2, :]
    if base == 0:
        pieces[0], others[0] = pieces[0].at[pl.ds(0, OWN_ROWS), :], others[0].at[pl.ds(OWN_ROWS, OWN_ROWS), :]
    xhat_out, cot_out, qg_out, kv_out, normed, cots = refs[-6:]
    width = weight.shape[0] // 4
    for n, piece in enumerate(pieces):
        here, there = pl.ds(n * OWN_ROWS, OWN_ROWS), pl.ds(base + n * OWN_ROWS, OWN_ROWS)
        xhat, _ = normalise(piece[...])
        xhat_out[there, :] = xhat.astype(BF16)
        normed[here, :] = (xhat * gain + bias).astype(BF16)
        cot_out[there, :] = others[n][...]
        cots[here, :] = others[n][...]
    packed = dot(normed[...], weight[: 3 * width, :], NT)
    queries = packed[:, :width].astype(BF16).astype(F32) * (1.0 / math.sqrt(width))
    there = pl.ds(base, count * OWN_ROWS)
    qg_out[there, :width] = queries.astype(BF16)
    kv_out[there, :] = packed[:, width:].astype(BF16)
    qg_out[there, width:] = dot(cots[...], weight[3 * width :, :], NT).astype(BF16)


def project(base, pieces, others, weight, norm, rows, before):
    count = len(pieces)
    total = count * OWN_ROWS
    width, model = weight.shape[0] // 4, weight.shape[1]
    first = 2 + 2 * count
    return pl.pallas_call(
        functools.partial(project_kernel, base, count),
        out_shape=(
            jax.ShapeDtypeStruct((rows, model), BF16),
            jax.ShapeDtypeStruct((rows, model), BF16),
            jax.ShapeDtypeStruct((rows, 2 * width), BF16),
            jax.ShapeDtypeStruct((rows, 2 * width), BF16),
        ),
        in_specs=[WHOLE] * (first + len(before)),
        out_specs=(WHOLE,) * 4,
        scratch_shapes=[pltpu.VMEM((total, model), BF16)] * 2,
        input_output_aliases={first + n: n for n in range(len(before))},
        name="project",
        **params(16, 2 * total * model * 4 * width, 4 * total * model * 2),
    )(*pieces, *others, weight, norm, *before)


def order_kernel(*refs):
    count = len(refs) // 4
    swap = lax.axis_index("blk") >= XN
    for n in range(count):
        own, other = refs[n][...], refs[count + n][...]
        refs[2 * count + n][...] = jnp.where(swap, other, own)
        refs[3 * count + n][...] = jnp.where(swap, own, other)


def order(own, other):
    count = len(own)
    out = pl.pallas_call(
        order_kernel,
        out_shape=[jax.ShapeDtypeStruct(v.shape, v.dtype) for v in own] * 2,
        in_specs=[WHOLE] * (2 * count),
        out_specs=[WHOLE] * (2 * count),
        name="order",
        **params(8, own[0].size, 8 * own[0].size),
    )(*own, *other)
    return out[:count], out[count:]


def forward_kernel(count, first, *refs):
    blocks = refs[:count]
    q_ref = refs[count]
    rest = refs[count + 1 :]
    if first:
        top = total = part = None
    else:
        top, total, part = rest[0][...], rest[1][...], rest[2][...]
        rest = rest[3:]
    m_out, l_out, acc_out = rest[:3]
    p_out, step_out = rest[3 : 3 + count], rest[3 + count : 3 + 2 * count]
    width = q_ref.shape[1] // 2
    queries = q_ref[:, :width]
    kvs, ahead = [], []
    for n in range(count + 1):
        if n < count:
            kvs.append(blocks[n][...])
            ahead.append(dot(kvs[n][:, :width], queries, NT))
        if n == 0:
            continue
        n, kv, scores = n - 1, kvs[n - 1], ahead[n - 1]
        new = jnp.max(scores, axis=0, keepdims=True)
        if top is not None:
            new = jnp.maximum(top, new)
        probs = jnp.exp(scores - new)
        weights = probs.astype(BF16)
        p_out[n][...] = weights
        step_out[n][...] = new
        sums = jnp.sum(probs, axis=0, keepdims=True)
        values = dot(kv[:, width:], weights, TN)
        if top is None:
            total, part = sums, values
        else:
            shrink = jnp.exp(top - new)
            total, part = total * shrink + sums, part * shrink + values
        top = new
    m_out[...], l_out[...], acc_out[...] = top, total, part


def forward(blocks, queries, state):
    count = len(blocks)
    rows, width = queries.shape[0], queries.shape[1] // 2
    keys = blocks[0].shape[0]
    first = state is None
    states = [(1, rows), (1, rows), (width, rows)]
    out = pl.pallas_call(
        functools.partial(forward_kernel, count, first),
        out_shape=[jax.ShapeDtypeStruct(s, F32) for s in states]
        + [jax.ShapeDtypeStruct((keys, rows), BF16)] * count
        + [jax.ShapeDtypeStruct((1, rows), F32)] * count,
        in_specs=[WHOLE] * (count + 1 + (0 if first else 3)),
        out_specs=[WHOLE] * (3 + 2 * count),
        name="forward",
        **params(
            24,
            count * 16 * rows * keys * width, count * 2 * rows * keys, count * rows * keys
        ),
    )(*blocks, queries, *([] if first else state))
    return out[:3], out[3 : 3 + count], out[3 + count :]


def split_thrice(value):
    high = value.astype(BF16).astype(F32)
    rest = value - high
    middle_part = rest.astype(BF16).astype(F32)
    return [high, middle_part, rest - middle_part]


def message_kernel(top, total, part, out):
    width, rows = part.shape
    out[:width, :] = part[...].astype(BF16)
    coded = split_thrice(top[...]) + split_thrice(total[...])
    coded = jnp.concatenate(coded + [jnp.zeros((10, rows), F32)], 0)
    out[width:, :] = coded.astype(BF16)


def message(top, total, part):
    width, rows = part.shape
    return pl.pallas_call(
        message_kernel,
        out_shape=jax.ShapeDtypeStruct((width + 16, rows), BF16),
        in_specs=[WHOLE] * 3,
        out_specs=WHOLE,
        name="message",
        **params(8, 4 * rows * width, 6 * rows * width),
    )(top, total, part)


def middle_kernel(top, total, part, got, qg, *refs):
    width = part.shape[0]
    earlier = refs[0] if len(refs) == 5 else None
    att_t, lse, delta = refs[1:4] if earlier is not None else refs
    coded = got[width:, :].astype(F32)
    their_top = coded[0:1] + coded[1:2] + coded[2:3]
    their_total = coded[3:4] + coded[4:5] + coded[5:6]
    new = jnp.maximum(top[...], their_top)
    mine, theirs = jnp.exp(top[...] - new), jnp.exp(their_top - new)
    both = total[...] * mine + their_total * theirs
    summed = part[...] * mine + got[:width, :].astype(F32) * theirs
    lse[...] = new + jnp.log(both)
    attended = (summed / both).astype(BF16)
    wide = attended.astype(F32)
    back = jnp.transpose(qg[:, width:].astype(F32), (1, 0))
    delta[...] = jnp.sum(back * wide, axis=0, keepdims=True)
    if earlier is not None:
        wide = jnp.where(lax.axis_index("blk") >= XN, wide, earlier[...].astype(F32))
        refs[-1][...] = jnp.transpose(wide, (1, 0)).astype(BF16)
    att_t[...] = wide.astype(BF16)


def regroup(rows, kept, sib, pair, diag):
    z, _ = position()
    width = rows.shape[1]
    for r in range(ZN // 2):
        to = pl.ds(r * OWN_ROWS, OWN_ROWS)
        for flip, near, far in ((0, kept, pair), (1, sib, diag)):
            near[to, :width] = rows[pl.ds(PLACE[2 * r, flip], OWN_ROWS), :]
            up, down = PLACE[(2 * r + 1) % ZN, flip], PLACE[(2 * r - 1) % ZN, flip]
            at = pl.multiple_of(jnp.where(lax.rem(z, 2) == 0, up, down), OWN_ROWS)
            far[to, :width] = rows[pl.ds(at, OWN_ROWS), :]


def middle(state, got, qg, earlier):
    width, rows = state[2].shape
    row = jax.ShapeDtypeStruct((1, rows), F32)
    last = earlier is not None
    att = (jax.ShapeDtypeStruct((rows, width), BF16),) if last else ()
    return pl.pallas_call(
        middle_kernel,
        out_shape=(jax.ShapeDtypeStruct((width, rows), BF16), row, row) + att,
        in_specs=[WHOLE] * (6 if last else 5),
        out_specs=(WHOLE,) * (4 if last else 3),
        name="middle",
        **params(16, 10 * rows * width, 8 * rows * width),
    )(*state, got, qg, *([earlier] if last else []))


def backward_kernel(own, has_dq, has_dkv, kv, *refs):
    count = 1 if own is None else 2
    stored, top = refs[:2]
    qgs, lses, deltas = (refs[2 + n * count : 2 + (n + 1) * count] for n in range(3))
    rest = refs[2 + 3 * count :]
    dq_in = rest[:count] if has_dq else None
    rest = rest[count:] if has_dq else rest
    dkv_in = rest[0] if has_dkv else None
    out, dq_out = rest[-2:]

    def pick(pair, *at):
        if own is None:
            return pair[0][at]
        swap = lax.axis_index("blk") >= XN
        first, second = pair if own else (pair[1], pair[0])
        return jnp.where(swap, second[at], first[at])

    width = kv.shape[1] // 2
    tile = 512
    dk = dkv_in[:, :width] if has_dkv else 0
    dv = dkv_in[:, width:] if has_dkv else 0
    for t in range(kv.shape[0] // tile):
        here = pl.ds(t * tile, tile)
        every = slice(None)
        qg = pick(qgs, here, every)
        q, grad = qg[:, :width], qg[:, width:]
        factor = jnp.exp(top[:, here] - pick(lses, every, here))
        prob_grad = dot(kv[:, width:], grad, NT)
        probs = stored[:, here].astype(F32) * factor
        score_grad = (probs * (prob_grad - pick(deltas, every, here))).astype(BF16)
        dv += dot(probs.astype(BF16), grad)
        dk += dot(score_grad, q)
        dq = dot(kv[:, :width], score_grad, TN)
        if has_dq:
            dq += pick(dq_in, every, here)
        dq_out[:, here] = dq.astype(dq_out.dtype)
    out[:, :width] = dk.astype(out.dtype)
    out[:, width:] = dv.astype(out.dtype)


def backward(own, kv, stored, top, qgs, lses, deltas, dqs, dkv, kinds):
    rows, width = qgs[0].shape[0], qgs[0].shape[1] // 2
    keys = kv.shape[0]
    given = ([] if dqs is None else list(dqs)) + ([] if dkv is None else [dkv])
    operands = [kv, stored, top, *qgs, *lses, *deltas, *given]
    return pl.pallas_call(
        functools.partial(backward_kernel, own, dqs is not None, dkv is not None),
        out_shape=[
            jax.ShapeDtypeStruct((keys, 2 * width), kinds[0]),
            jax.ShapeDtypeStruct((width, rows), kinds[1]),
        ],
        in_specs=[WHOLE] * len(operands),
        out_specs=[WHOLE] * 2,
        name="backward",
        **params(24, 32 * rows * keys * width, 2 * rows * keys),
    )(*operands)


def out_kernel(att_t, cot, part, sums):
    part[...] = dot(att_t[...], cot[...]).astype(BF16)
    sums[...] = jnp.sum(cot[...].astype(F32), axis=0, keepdims=True)


def out_sums(att_t, cot):
    return pl.pallas_call(
        out_kernel,
        out_shape=(
            jax.ShapeDtypeStruct((att_t.shape[0], cot.shape[1]), BF16),
            jax.ShapeDtypeStruct((1, cot.shape[1]), F32),
        ),
        in_specs=[WHOLE] * 2,
        out_specs=(WHOLE,) * 2,
        name="out_sums",
        **params(16, 2 * att_t.size * cot.shape[1], 2 * cot.size),
    )(att_t, cot)


def split_rows(value):
    high = value.astype(BF16).astype(F32)
    return [high, value - high]


def collect_kernel(dq, dq_part, own, att, out_part, xhat, weight, gain, bias, *refs):
    parts = refs[:3]
    grad, *targets = refs[3:7]
    wide, kept, sib, far, sems = refs[7:]
    height = kept.shape[0]
    pair, diag = far.at[pl.ds(0, height), :], far.at[pl.ds(height, height), :]
    width = dq.shape[0]
    total = own[...]
    for part in parts:
        total = total + part[...].astype(F32)
    query = dq[...] + dq_part[...].astype(F32)
    query = jnp.transpose(query * (1.0 / math.sqrt(width)), (1, 0))
    packed = jnp.concatenate([query, total], 1).astype(BF16)
    wide[:, : 3 * width] = packed
    wide[:, 3 * width :] = att[...]
    regroup(wide, kept, sib, pair, diag)
    moment = dot(packed, xhat[...], TN)
    flipped = jnp.transpose(packed.astype(F32), (1, 0))
    sums = jnp.sum(flipped, axis=1, keepdims=True)
    grad[: 3 * width, :] = (moment * gain[...] + sums * bias[...]).astype(BF16)
    grad[3 * width :, :] = out_part[...]
    held = weight[: 3 * width, :].astype(F32)
    rows = split_rows(jnp.sum(held * moment, axis=0, keepdims=True))
    rows += split_rows(jnp.sum(held * sums, axis=0, keepdims=True))
    coded = [row[:, n * 256 : (n + 1) * 256] for row in rows for n in range(4)]
    coded = jnp.concatenate(coded, 0).astype(BF16)
    for target in (kept, sib, pair, diag):
        target[256:, :] = coded
    fetch((kept, sib, far), targets, sems, True)


def collect(dq, dq_part, own, att, out_part, xhat, weight, gain, bias, parts):
    width, rows = dq.shape
    quarter = jax.ShapeDtypeStruct((rows // 4 + 16, 256), BF16)
    double = jax.ShapeDtypeStruct((2 * (rows // 4 + 16), 256), BF16)
    return pl.pallas_call(
        collect_kernel,
        out_shape=(jax.ShapeDtypeStruct(weight.shape, BF16), quarter, quarter, double),
        in_specs=[WHOLE] * 12,
        out_specs=(WHOLE, HBM, HBM, HBM),
        scratch_shapes=[pltpu.VMEM((rows, 4 * width), BF16)] + room([quarter, quarter, double]),
        name="collect",
        **params(16, 8 * weight.size * rows, 24 * rows * width),
    )(dq, dq_part, own, att, out_part, xhat, weight, gain, bias, *parts)


def spread_kernel(*refs):
    own, vectors_out, up, down, near_up, near_down = refs[8:14]
    held, sems = refs[14:22], refs[22]
    height = refs[0].shape[0]
    sources = [refs[0], refs[1], refs[2].at[pl.ds(0, height), :], refs[3].at[pl.ds(height, height), :]]
    ready = fetch([*sources, *refs[4:8]], held, sems)
    depth = 3 * refs[4].shape[0] // 4
    total = laid = coded = 0
    for n in range(4):
        piece, weight = ready(n), ready(4 + n)
        total += dot(piece[:256, :depth], weight[:depth, :])
        laid += dot(piece[:256, depth:], weight[depth:, :])
        coded += piece[256:, :].astype(F32)
    vectors = []
    for v in range(2):
        row = coded[8 * v : 8 * v + 4] + coded[8 * v + 4 : 8 * v + 8]
        vectors.append(jnp.concatenate([row[n : n + 1] for n in range(4)], 1))
    rows = split_rows(vectors[0]) + split_rows(vectors[1])
    rows = jnp.concatenate(rows + [jnp.zeros((4, rows[0].shape[1]), F32)], 0).astype(BF16)
    own[:64, :], own[64:, :] = total[:64], laid[:64]
    vectors_out[...] = rows
    up[:64, :], down[:64, :] = total[128:192].astype(BF16), laid[128:192].astype(BF16)
    up[64:, :], down[64:, :] = rows, rows
    near_up[:64, :], near_up[64:, :] = total[64:128].astype(BF16), laid[64:128].astype(BF16)
    near_down[:64, :], near_down[64:, :] = total[192:].astype(BF16), laid[192:].astype(BF16)


def spread(pieces, weights):
    model = weights[0].shape[1]
    shape = lambda rows, kind: jax.ShapeDtypeStruct((rows, model), kind)
    height = pieces[0].shape
    held = [jax.ShapeDtypeStruct(height, BF16)] * 4
    return pl.pallas_call(
        spread_kernel,
        out_shape=[
            shape(128, F32),
            shape(8, BF16),
            shape(72, BF16),
            shape(72, BF16),
            shape(128, BF16),
            shape(128, BF16),
        ],
        in_specs=[HBM] * 8,
        out_specs=[WHOLE] * 6,
        scratch_shapes=room([*held, *weights]),
        name="spread",
        **params(60, 8 * 256 * 768 * 1024, 2 * 4 * weights[0].size),
    )(*pieces, *weights)


def relay_kernel(got_up, got_down, near_up, near_down, up, down):
    up[:64, :] = (near_up[:64, :].astype(F32) + got_up[:64, :].astype(F32)).astype(BF16)
    up[64:, :] = near_up[64:, :]
    down[:64, :] = near_down[:64, :]
    down[64:, :] = (near_down[64:, :].astype(F32) + got_down[:64, :].astype(F32)).astype(BF16)


def relay(got_up, got_down, near_up, near_down):
    model = got_up.shape[1]
    return pl.pallas_call(
        relay_kernel,
        out_shape=[jax.ShapeDtypeStruct((128, model), BF16)] * 2,
        in_specs=[WHOLE] * 4,
        out_specs=[WHOLE] * 2,
        name="relay",
        **params(8, got_up.size, 8 * got_up.size),
    )(got_up, got_down, near_up, near_down)


def finish_kernel(tokens, cot, gain, out_bias, own, up, down, grad_out, layer_out):
    normed_grad = own[:64, :] + up[:64, :].astype(F32) + down[:64, :].astype(F32)
    xhat, inverse = normalise(tokens[...])
    scaled = normed_grad * gain[...]
    simple = jnp.mean(scaled, axis=-1, keepdims=True)
    product = jnp.mean(scaled * xhat, axis=-1, keepdims=True)
    grad = cot[...].astype(F32) + inverse * (scaled - simple - xhat * product)
    grad_out[...] = grad.astype(BF16)
    laid = own[64:, :] + up[64:, :].astype(F32) + down[64:, :].astype(F32)
    layer_out[...] = (tokens[...].astype(F32) + laid + out_bias[...]).astype(BF16)


def finish(tokens, cot, gain, out_bias, own, up, down):
    return pl.pallas_call(
        finish_kernel,
        out_shape=[jax.ShapeDtypeStruct(tokens.shape, BF16)] * 2,
        in_specs=[WHOLE] * 7,
        out_specs=[WHOLE] * 2,
        name="finish",
        **params(16, 20 * tokens.size, 12 * tokens.size),
    )(tokens, cot, gain, out_bias, own, up, down)


def add_kernel(factor, got, bias_sum, *refs):
    coded, out = refs[:4], refs[4]
    total = got[0].astype(F32)
    for n in range(1, got.shape[0]):
        total += got[n].astype(F32)
    height = total.shape[0]
    part = (total * factor).astype(BF16)
    rows = 0
    for ref in coded:
        rows += ref[ref.shape[0] - 8 :, :].astype(F32)
    vectors = split_rows(rows[0:1] + rows[1:2]) + split_rows(rows[2:3] + rows[3:4])
    vectors += split_rows(bias_sum[...])
    vectors = jnp.concatenate(vectors + [jnp.zeros((2, total.shape[1]), F32)], 0)
    vectors = vectors.astype(BF16)
    for n in range(out.shape[0]):
        out[n, :height, :] = part
        out[n, height:, :] = vectors


def add(got, bias_sum, coded, factor):
    ways, height, model = got.shape
    return pl.pallas_call(
        functools.partial(add_kernel, factor),
        out_shape=jax.ShapeDtypeStruct((ways, height + 8, model), BF16),
        in_specs=[WHOLE] * 6,
        out_specs=WHOLE,
        name="add",
        **params(16, got.size, 2 * got.size),
    )(got, bias_sum, *coded)


def unpack_kernel(factor, every, qkv, out, bias, gain, shift):
    ways = every.shape[0]
    height = 4 * out.shape[0] // ways
    each = ways // 4
    total = 0
    for n in range(ways):
        rows = every[n, :height, :].astype(F32)
        here = pl.ds((n % each) * height, height)
        if n // each < 3:
            qkv[n // each, here, :] = rows
        else:
            out[here, :] = rows
        total += every[n, height:, :].astype(F32)
    total *= factor
    gain[...] = total[0:1] + total[1:2]
    shift[...] = total[2:3] + total[3:4]
    bias[...] = total[4:5] + total[5:6]


def unpack(every, width, factor):
    model = every.shape[2]
    vector = jax.ShapeDtypeStruct((1, model), F32)
    return pl.pallas_call(
        functools.partial(unpack_kernel, factor),
        out_shape=(
            jax.ShapeDtypeStruct((3, width, model), F32),
            jax.ShapeDtypeStruct((width, model), F32),
            vector,
            vector,
            vector,
        ),
        in_specs=[WHOLE],
        out_specs=(WHOLE,) * 5,
        name="unpack",
        **params(8, every.size, 6 * every.size),
    )(every)


def tie(value, *others):
    return lax.optimization_barrier((value,) + others)[0]


def on_device(
    tokens, cotangent, qkv_weight, out_weight, out_bias, norm_gain_vector, norm_bias_vector
):
    own_tokens = tokens[0]
    own_cot = cotangent[0]
    own_rows, model = own_tokens.shape
    width = qkv_weight.shape[1]
    weight = jnp.concatenate([qkv_weight.reshape(3 * width, model), out_weight], 0)
    gain = norm_gain_vector[None]
    bias = norm_bias_vector[None]
    rows = HEADS * own_rows

    right, left, cot_right, cot_left = own_tokens, own_tokens, own_cot, own_cot
    both = jnp.concatenate([own_tokens, own_cot], 0)
    norm = jnp.concatenate([gain, bias], 0)
    pieces, others = [both, to_sibling(own_tokens)], [both, to_sibling(own_cot)]
    early = None
    for steps in (1, 2, 3):
        right, left = along_z(right, 1), along_z(left, -1)
        cot_right, cot_left = along_z(cot_right, 1), along_z(cot_left, -1)
        if steps == 1:
            right, weight, norm, both = lax.optimization_barrier((right, weight, norm, both))
            pieces[0] = others[0] = both
        pieces += [right, left, to_sibling(right), to_sibling(left)]
        others += [cot_right, cot_left, to_sibling(cot_right), to_sibling(cot_left)]
        if steps == 2:
            early = project(0, pieces, others, weight, norm, rows, [])
            pieces, others = [], []
    right, cot_left = along_z(right, 1), along_z(cot_left, -1)
    right, *early = lax.optimization_barrier((right, *early))
    pieces += [right, to_sibling(right)]
    others += [cot_left, to_sibling(cot_left)]
    xhat, cot_all, own_qg, own_kv = project(
        len(EARLY) * OWN_ROWS, pieces, others, weight, norm, rows, early
    )

    other_qg = to_half(own_qg)
    arrived = [along_x(own_kv, steps) for steps in OFFSETS[:2]]
    other_qg, arrived[0], arrived[1], held_kv = lax.optimization_barrier(
        (other_qg, arrived[0], arrived[1], own_kv)
    )
    arrived.append(along_x(held_kv, OFFSETS[2]))
    own_state, own_probs, own_top = forward([own_kv], own_qg, None)
    other_state, other_probs, other_top = forward([held_kv], other_qg, None)
    first, second = order([own_qg, *own_state], [other_qg, *other_state])
    qgs = [first[0], second[0]]
    states = [first[1:], second[1:]]
    stored, tops, lses, deltas = [[], []], [[], []], [None, None], [None, None]
    got = [None, None]
    for n, wave in ((0, arrived[:2]), (1, arrived[:2]), (0, arrived[2:]), (1, arrived[2:])):
        states[n], probs, top = forward(wave, qgs[n], states[n])
        stored[n] += probs
        tops[n] += top
        if len(wave) == 1:
            got[n] = to_half(message(*states[n]))
        if n == 0:
            *states[0], qgs[1] = lax.optimization_barrier((*states[0], qgs[1]))
        elif len(wave) == 2:
            later_weight = tie(weight, states[1][0])
            w_pair, w_sib = to_pair(later_weight), to_sibling(later_weight)
            *states[1], qgs[0] = lax.optimization_barrier((*states[1], qgs[0]))

    early_att, lses[0], deltas[0] = middle(states[0], got[0], qgs[0], None)
    dqs = [None, None]
    far = (2, 0, 1)
    parts = {}
    home = []
    for n in range(2):
        if n == 1:
            got[1], dqs[0] = lax.optimization_barrier((got[1], dqs[0]))
            w_diag = to_sibling(w_pair)
            w_sib, w_pair, dqs[0] = lax.optimization_barrier((w_sib, w_pair, dqs[0]))
            att_t, lses[1], deltas[1], att = middle(states[1], got[1], qgs[1], early_att)
        for k in far:
            parts[k], dqs[n] = backward(
                None,
                arrived[k],
                stored[n][k],
                tops[n][k],
                [qgs[n]],
                [lses[n]],
                [deltas[n]],
                None if dqs[n] is None else [dqs[n]],
                None if n == 0 else parts[k],
                (F32 if n == 0 else BF16, F32),
            )
            if n == 1:
                home.append(along_x(parts[k], -OFFSETS[k]))
    own_part = None
    last = [None, None]
    for own in (False, True):
        own_part, last[own] = backward(
            own,
            own_kv,
            own_probs[0] if own else other_probs[0],
            own_top[0] if own else other_top[0],
            qgs,
            lses,
            deltas,
            dqs,
            own_part,
            (F32, F32 if own else BF16),
        )
        if not own:
            dq_part = to_half(last[0])
            home[0], own_part = lax.optimization_barrier((home[0], own_part))
    out_part, bias_sum = out_sums(tie(att_t, last[1]), cot_all)

    matrix, kept, sib, far = collect(
        last[1], dq_part, own_part, att, out_part, xhat, weight, gain, bias, home
    )
    sib, far = to_sibling(sib), to_pair(far)
    near = to_sibling(far)
    own, coded, up, down, *nearest = spread(
        (kept, sib, far, near), (weight, w_sib, w_pair, w_diag)
    )
    got_up, got_down, got_coded = along_z(up, 2), along_z(down, -2), along_z(coded, 4)
    up, down = relay(got_up, got_down, *nearest)

    ways = lax.axis_size("dp") * lax.axis_size("blk")
    factor = 1.0 / math.sqrt(ways * rows)
    matrix = tie(matrix, sib).reshape(ways, 4 * width // ways, model)
    got = lax.all_to_all(matrix, ("dp", "blk"), 0, 0, tiled=True)
    got, up, down = lax.optimization_barrier((got, up, down))
    back = add(got, bias_sum, (coded, got_up, got_down, got_coded), factor)
    every = lax.all_to_all(back, ("dp", "blk"), 0, 0, tiled=True)
    grad_rows, layer_rows = finish(
        own_tokens, own_cot, gain, out_bias[None], own, along_z(up, 2), along_z(down, -2)
    )
    qkv_grad, out_grad, bias_grad, gain_grad, shift_grad = unpack(every, width, factor)
    return (
        layer_rows[None],
        grad_rows[None],
        qkv_grad,
        out_grad,
        bias_grad[0],
        gain_grad[0],
        shift_grad[0],
    )


def solution(mesh):
    tokens = P("dp", ("head", "blk"), None)
    heads = P("head", None)
    return jax.shard_map(
        on_device,
        mesh=mesh,
        in_specs=(tokens, tokens, P(None, "head", None), heads, P(), P(), P()),
        out_specs=(tokens, tokens, P(None, "head", None), heads, P(), P(), P()),
        check_vma=False,
    )
```

```python
import functools
import math

import jax
import jax.numpy as jnp
from jax import lax
from jax.experimental import pallas as pl
from jax.experimental.pallas import tpu as pltpu
from jax.sharding import PartitionSpec as P

HEADS = 16
EPSILON = 1e-06
ZN = 8
XN = 4
F32 = jnp.float32
BF16 = jnp.bfloat16
WHOLE = pl.BlockSpec(memory_space=pltpu.VMEM)
HBM = pl.BlockSpec(memory_space=pltpu.HBM)
NT = (((1,), (1,)), ((), ()))
TN = (((0,), (0,)), ((), ()))
NN = (((1,), (0,)), ((), ()))

OFFSETS = (1, 3, 2)

EARLY = ((0, 0), (0, 1), (-1, 0), (1, 0), (-1, 1), (1, 1), (-2, 0), (2, 0), (-2, 1), (2, 1))
LATE = ((-3, 0), (3, 0), (-3, 1), (3, 1), (4, 0), (4, 1))
OWN_ROWS = 64
PLACE = {(steps % ZN, flip): n * OWN_ROWS for n, (steps, flip) in enumerate(EARLY + LATE)}


def dot(a, b, dims=NN):
    return lax.dot_general(a, b, dims, preferred_element_type=F32)


def params(mib, flops=0, moved=0, trans=0):
    return dict(
        compiler_params=pltpu.CompilerParams(vmem_limit_bytes=mib * 2**20),
        cost_estimate=pl.CostEstimate(flops=flops, bytes_accessed=moved, transcendentals=trans),
    )


def permute(value, axis, count, target):
    return lax.ppermute(value, axis, [(i, target(i)) for i in range(count)])


def along_z(value, steps):
    return permute(value, "head", HEADS, lambda h: ((h // 2 + steps) % ZN) * 2 + h % 2)


def to_sibling(value):
    return permute(value, "head", HEADS, lambda h: h ^ 1)


def to_pair(value):
    return permute(value, "head", HEADS, lambda h: h ^ 2)


def to_diagonal(value):
    return permute(value, "head", HEADS, lambda h: h ^ 3)


def along_x(value, steps):
    return permute(value, "blk", 2 * XN, lambda b: (b // XN) * XN + (b % XN + steps) % XN)


def to_half(value):
    return permute(value, "blk", 2 * XN, lambda b: b ^ XN)


def fetch(sources, held, sems, finish_all=False):
    copies = [pltpu.make_async_copy(a, b, sems.at[n]) for n, (a, b) in enumerate(zip(sources, held))]
    for copy in copies:
        copy.start()

    if finish_all:
        for copy in copies:
            copy.wait()

    def ready(n):
        copies[n].wait()
        return held[n]

    return ready


def room(values):
    return [pltpu.VMEM(v.shape, v.dtype) for v in values] + [
        pltpu.SemaphoreType.DMA((len(values),))
    ]


def position():
    head = lax.axis_index("head")
    return head // 2, lax.rem(head, 2)


def normalise(rows):
    values = rows.astype(F32)
    shifted = values - jnp.mean(values, axis=-1, keepdims=True)
    spread = jnp.mean(shifted * shifted, axis=-1, keepdims=True)
    inverse = lax.rsqrt(spread + EPSILON)
    return shifted * inverse, inverse


def project_kernel(base, count, *refs):
    pieces, others = list(refs[:count]), list(refs[count : 2 * count])
    weight, norm = refs[2 * count : 2 * count + 2]
    gain, bias = norm[0:1, :], norm[1:2, :]
    if base == 0:
        pieces[0], others[0] = pieces[0].at[pl.ds(0, OWN_ROWS), :], others[0].at[pl.ds(OWN_ROWS, OWN_ROWS), :]
    xhat_out, cot_out, qg_out, kv_out, normed, cots = refs[-6:]
    width = weight.shape[0] // 4
    for n, piece in enumerate(pieces):
        here, there = pl.ds(n * OWN_ROWS, OWN_ROWS), pl.ds(base + n * OWN_ROWS, OWN_ROWS)
        xhat, _ = normalise(piece[...])
        xhat_out[there, :] = xhat.astype(BF16)
        normed[here, :] = (xhat * gain + bias).astype(BF16)
        cot_out[there, :] = others[n][...]
        cots[here, :] = others[n][...]
    packed = dot(normed[...], weight[: 3 * width, :], NT)
    queries = packed[:, :width].astype(BF16).astype(F32) * (1.0 / math.sqrt(width))
    there = pl.ds(base, count * OWN_ROWS)
    qg_out[there, :width] = queries.astype(BF16)
    kv_out[there, :] = packed[:, width:].astype(BF16)
    qg_out[there, width:] = dot(cots[...], weight[3 * width :, :], NT).astype(BF16)


def project(base, pieces, others, weight, norm, rows, before):
    count = len(pieces)
    total = count * OWN_ROWS
    width, model = weight.shape[0] // 4, weight.shape[1]
    first = 2 + 2 * count
    return pl.pallas_call(
        functools.partial(project_kernel, base, count),
        out_shape=(
            jax.ShapeDtypeStruct((rows, model), BF16),
            jax.ShapeDtypeStruct((rows, model), BF16),
            jax.ShapeDtypeStruct((rows, 2 * width), BF16),
            jax.ShapeDtypeStruct((rows, 2 * width), BF16),
        ),
        in_specs=[WHOLE] * (first + len(before)),
        out_specs=(WHOLE,) * 4,
        scratch_shapes=[pltpu.VMEM((total, model), BF16)] * 2,
        input_output_aliases={first + n: n for n in range(len(before))},
        name="project",
        **params(16, 2 * total * model * 4 * width, 4 * total * model * 2),
    )(*pieces, *others, weight, norm, *before)


def order_kernel(*refs):
    count = len(refs) // 4
    swap = lax.axis_index("blk") >= XN
    for n in range(count):
        own, other = refs[n][...], refs[count + n][...]
        refs[2 * count + n][...] = jnp.where(swap, other, own)
        refs[3 * count + n][...] = jnp.where(swap, own, other)


def order(own, other):
    count = len(own)
    out = pl.pallas_call(
        order_kernel,
        out_shape=[jax.ShapeDtypeStruct(v.shape, v.dtype) for v in own] * 2,
        in_specs=[WHOLE] * (2 * count),
        out_specs=[WHOLE] * (2 * count),
        name="order",
        **params(8, own[0].size, 8 * own[0].size),
    )(*own, *other)
    return out[:count], out[count:]


def forward_kernel(count, first, *refs):
    blocks = refs[:count]
    q_ref = refs[count]
    rest = refs[count + 1 :]
    if first:
        top = total = part = None
    else:
        top, total, part = rest[0][...], rest[1][...], rest[2][...]
        rest = rest[3:]
    m_out, l_out, acc_out = rest[:3]
    p_out, step_out = rest[3 : 3 + count], rest[3 + count : 3 + 2 * count]
    width = q_ref.shape[1] // 2
    queries = q_ref[:, :width]
    kvs, ahead = [], []
    for n in range(count + 1):
        if n < count:
            kvs.append(blocks[n][...])
            ahead.append(dot(kvs[n][:, :width], queries, NT))
        if n == 0:
            continue
        n, kv, scores = n - 1, kvs[n - 1], ahead[n - 1]
        new = jnp.max(scores, axis=0, keepdims=True)
        if top is not None:
            new = jnp.maximum(top, new)
        probs = jnp.exp(scores - new)
        weights = probs.astype(BF16)
        p_out[n][...] = weights
        step_out[n][...] = new
        sums = jnp.sum(probs, axis=0, keepdims=True)
        values = dot(kv[:, width:], weights, TN)
        if top is None:
            total, part = sums, values
        else:
            shrink = jnp.exp(top - new)
            total, part = total * shrink + sums, part * shrink + values
        top = new
    m_out[...], l_out[...], acc_out[...] = top, total, part


def forward(blocks, queries, state):
    count = len(blocks)
    rows, width = queries.shape[0], queries.shape[1] // 2
    keys = blocks[0].shape[0]
    first = state is None
    states = [(1, rows), (1, rows), (width, rows)]
    out = pl.pallas_call(
        functools.partial(forward_kernel, count, first),
        out_shape=[jax.ShapeDtypeStruct(s, F32) for s in states]
        + [jax.ShapeDtypeStruct((keys, rows), BF16)] * count
        + [jax.ShapeDtypeStruct((1, rows), F32)] * count,
        in_specs=[WHOLE] * (count + 1 + (0 if first else 3)),
        out_specs=[WHOLE] * (3 + 2 * count),
        name="forward",
        **params(
            24,
            count * 16 * rows * keys * width, count * 2 * rows * keys, count * rows * keys
        ),
    )(*blocks, queries, *([] if first else state))
    return out[:3], out[3 : 3 + count], out[3 + count :]


def split_thrice(value):
    high = value.astype(BF16).astype(F32)
    rest = value - high
    middle_part = rest.astype(BF16).astype(F32)
    return [high, middle_part, rest - middle_part]


def message_kernel(top, total, part, out):
    width, rows = part.shape
    out[:width, :] = part[...].astype(BF16)
    coded = split_thrice(top[...]) + split_thrice(total[...])
    coded = jnp.concatenate(coded + [jnp.zeros((10, rows), F32)], 0)
    out[width:, :] = coded.astype(BF16)


def message(top, total, part):
    width, rows = part.shape
    return pl.pallas_call(
        message_kernel,
        out_shape=jax.ShapeDtypeStruct((width + 16, rows), BF16),
        in_specs=[WHOLE] * 3,
        out_specs=WHOLE,
        name="message",
        **params(8, 4 * rows * width, 6 * rows * width),
    )(top, total, part)


def middle_kernel(top, total, part, got, qg, *refs):
    width = part.shape[0]
    earlier = refs[0] if len(refs) == 5 else None
    att_t, lse, delta = refs[1:4] if earlier is not None else refs
    coded = got[width:, :].astype(F32)
    their_top = coded[0:1] + coded[1:2] + coded[2:3]
    their_total = coded[3:4] + coded[4:5] + coded[5:6]
    new = jnp.maximum(top[...], their_top)
    mine, theirs = jnp.exp(top[...] - new), jnp.exp(their_top - new)
    both = total[...] * mine + their_total * theirs
    summed = part[...] * mine + got[:width, :].astype(F32) * theirs
    lse[...] = new + jnp.log(both)
    attended = (summed / both).astype(BF16)
    wide = attended.astype(F32)
    back = jnp.transpose(qg[:, width:].astype(F32), (1, 0))
    delta[...] = jnp.sum(back * wide, axis=0, keepdims=True)
    if earlier is not None:
        wide = jnp.where(lax.axis_index("blk") >= XN, wide, earlier[...].astype(F32))
        refs[-1][...] = jnp.transpose(wide, (1, 0)).astype(BF16)
    att_t[...] = wide.astype(BF16)


def regroup(rows, kept, sib, pair, diag):
    z, _ = position()
    width = rows.shape[1]
    for r in range(ZN // 2):
        to = pl.ds(r * OWN_ROWS, OWN_ROWS)
        for flip, near, far in ((0, kept, pair), (1, sib, diag)):
            near[to, :width] = rows[pl.ds(PLACE[2 * r, flip], OWN_ROWS), :]
            up, down = PLACE[(2 * r + 1) % ZN, flip], PLACE[(2 * r - 1) % ZN, flip]
            at = pl.multiple_of(jnp.where(lax.rem(z, 2) == 0, up, down), OWN_ROWS)
            far[to, :width] = rows[pl.ds(at, OWN_ROWS), :]


def middle(state, got, qg, earlier):
    width, rows = state[2].shape
    row = jax.ShapeDtypeStruct((1, rows), F32)
    last = earlier is not None
    att = (jax.ShapeDtypeStruct((rows, width), BF16),) if last else ()
    return pl.pallas_call(
        middle_kernel,
        out_shape=(jax.ShapeDtypeStruct((width, rows), BF16), row, row) + att,
        in_specs=[WHOLE] * (6 if last else 5),
        out_specs=(WHOLE,) * (4 if last else 3),
        name="middle",
        **params(16, 10 * rows * width, 8 * rows * width),
    )(*state, got, qg, *([earlier] if last else []))


def backward_kernel(own, has_dq, has_dkv, kv, *refs):
    count = 1 if own is None else 2
    stored, top = refs[:2]
    qgs, lses, deltas = (refs[2 + n * count : 2 + (n + 1) * count] for n in range(3))
    rest = refs[2 + 3 * count :]
    dq_in = rest[:count] if has_dq else None
    rest = rest[count:] if has_dq else rest
    dkv_in = rest[0] if has_dkv else None
    out, dq_out = rest[-2:]

    def pick(pair, *at):
        if own is None:
            return pair[0][at]
        swap = lax.axis_index("blk") >= XN
        first, second = pair if own else (pair[1], pair[0])
        return jnp.where(swap, second[at], first[at])

    width = kv.shape[1] // 2
    tile = 512
    dk = dkv_in[:, :width] if has_dkv else 0
    dv = dkv_in[:, width:] if has_dkv else 0
    for t in range(kv.shape[0] // tile):
        here = pl.ds(t * tile, tile)
        every = slice(None)
        qg = pick(qgs, here, every)
        q, grad = qg[:, :width], qg[:, width:]
        factor = jnp.exp(top[:, here] - pick(lses, every, here))
        prob_grad = dot(kv[:, width:], grad, NT)
        probs = stored[:, here].astype(F32) * factor
        score_grad = (probs * (prob_grad - pick(deltas, every, here))).astype(BF16)
        dv += dot(probs.astype(BF16), grad)
        dk += dot(score_grad, q)
        dq = dot(kv[:, :width], score_grad, TN)
        if has_dq:
            dq += pick(dq_in, every, here)
        dq_out[:, here] = dq.astype(dq_out.dtype)
    out[:, :width] = dk.astype(out.dtype)
    out[:, width:] = dv.astype(out.dtype)


def backward(own, kv, stored, top, qgs, lses, deltas, dqs, dkv, kinds):
    rows, width = qgs[0].shape[0], qgs[0].shape[1] // 2
    keys = kv.shape[0]
    given = ([] if dqs is None else list(dqs)) + ([] if dkv is None else [dkv])
    operands = [kv, stored, top, *qgs, *lses, *deltas, *given]
    return pl.pallas_call(
        functools.partial(backward_kernel, own, dqs is not None, dkv is not None),
        out_shape=[
            jax.ShapeDtypeStruct((keys, 2 * width), kinds[0]),
            jax.ShapeDtypeStruct((width, rows), kinds[1]),
        ],
        in_specs=[WHOLE] * len(operands),
        out_specs=[WHOLE] * 2,
        name="backward",
        **params(24, 32 * rows * keys * width, 2 * rows * keys),
    )(*operands)


def out_kernel(att_t, cot, part, sums):
    part[...] = dot(att_t[...], cot[...]).astype(BF16)
    sums[...] = jnp.sum(cot[...].astype(F32), axis=0, keepdims=True)


def out_sums(att_t, cot):
    return pl.pallas_call(
        out_kernel,
        out_shape=(
            jax.ShapeDtypeStruct((att_t.shape[0], cot.shape[1]), BF16),
            jax.ShapeDtypeStruct((1, cot.shape[1]), F32),
        ),
        in_specs=[WHOLE] * 2,
        out_specs=(WHOLE,) * 2,
        name="out_sums",
        **params(16, 2 * att_t.size * cot.shape[1], 2 * cot.size),
    )(att_t, cot)


def split_rows(value):
    high = value.astype(BF16).astype(F32)
    return [high, value - high]


def collect_kernel(dq, dq_part, own, att, out_part, xhat, weight, gain, bias, *refs):
    parts = refs[:3]
    grad, *targets = refs[3:7]
    wide, kept, sib, far, sems = refs[7:]
    height = kept.shape[0]
    pair, diag = far.at[pl.ds(0, height), :], far.at[pl.ds(height, height), :]
    width = dq.shape[0]
    total = own[...]
    for part in parts:
        total = total + part[...].astype(F32)
    query = dq[...] + dq_part[...].astype(F32)
    query = (query * (1.0 / math.sqrt(width))).astype(BF16).astype(F32)
    total = total.astype(BF16).astype(F32)
    packed = jnp.concatenate([jnp.transpose(query, (1, 0)), total], 1).astype(BF16)
    flipped = jnp.concatenate([query, jnp.transpose(total, (1, 0))], 0)
    wide[:, : 3 * width] = packed
    wide[:, 3 * width :] = att[...]
    regroup(wide, kept, sib, pair, diag)
    moment = dot(flipped.astype(BF16), xhat[...])
    sums = jnp.sum(flipped, axis=1, keepdims=True)
    grad[: 3 * width, :] = (moment * gain[...] + sums * bias[...]).astype(BF16)
    grad[3 * width :, :] = out_part[...]
    held = weight[: 3 * width, :].astype(F32)
    rows = split_rows(jnp.sum(held * moment, axis=0, keepdims=True))
    rows += split_rows(jnp.sum(held * sums, axis=0, keepdims=True))
    coded = [row[:, n * 256 : (n + 1) * 256] for row in rows for n in range(4)]
    coded = jnp.concatenate(coded, 0).astype(BF16)
    for target in (kept, sib, pair, diag):
        target[256:, :] = coded
    fetch((kept, sib, far), targets, sems, True)


def collect(dq, dq_part, own, att, out_part, xhat, weight, gain, bias, parts):
    width, rows = dq.shape
    quarter = jax.ShapeDtypeStruct((rows // 4 + 16, 256), BF16)
    double = jax.ShapeDtypeStruct((2 * (rows // 4 + 16), 256), BF16)
    return pl.pallas_call(
        collect_kernel,
        out_shape=(jax.ShapeDtypeStruct(weight.shape, BF16), quarter, quarter, double),
        in_specs=[WHOLE] * 12,
        out_specs=(WHOLE, HBM, HBM, HBM),
        scratch_shapes=[pltpu.VMEM((rows, 4 * width), BF16)] + room([quarter, quarter, double]),
        name="collect",
        **params(16, 8 * weight.size * rows, 24 * rows * width),
    )(dq, dq_part, own, att, out_part, xhat, weight, gain, bias, *parts)


def spread_kernel(*refs):
    bias_sum, own, vectors_out, up, down, near = refs[8:14]
    height = refs[0].shape[0]
    pieces = [refs[0], refs[1], refs[2].at[pl.ds(0, height), :], refs[3].at[pl.ds(height, height), :]]
    weights = refs[4:8]
    depth = 3 * refs[4].shape[0] // 4
    coded = sum(piece[256:, :].astype(F32) for piece in pieces)
    total = dot(
        jnp.concatenate([piece[:256, :depth] for piece in pieces], 1),
        jnp.concatenate([weight[:depth, :] for weight in weights], 0),
    )
    laid = dot(
        jnp.concatenate([piece[:256, depth:] for piece in pieces], 1),
        jnp.concatenate([weight[depth:, :] for weight in weights], 0),
    )
    vectors = []
    for v in range(2):
        row = coded[8 * v : 8 * v + 4] + coded[8 * v + 4 : 8 * v + 8]
        vectors.append(jnp.concatenate([row[n : n + 1] for n in range(4)], 1))
    rows = split_rows(vectors[0]) + split_rows(vectors[1])
    rows = jnp.concatenate(rows + [jnp.zeros((4, rows[0].shape[1]), F32)], 0).astype(BF16)
    own[:64, :], own[64:, :] = total[:64], laid[:64]
    vectors_out[...] = rows
    up[:64, :], down[:64, :] = total[128:192].astype(BF16), laid[128:192].astype(BF16)
    up[64:, :], down[64:, :] = rows, rows
    near[:64, :], near[64:128, :] = total[64:128].astype(BF16), laid[64:128].astype(BF16)
    near[128:192, :], near[192:256, :] = total[192:].astype(BF16), laid[192:].astype(BF16)
    sums = split_rows(bias_sum[...])
    sums = jnp.concatenate(sums + [jnp.zeros((6, sums[0].shape[1]), F32)], 0).astype(BF16)
    near[256:264, :], near[264:, :] = rows, sums


def spread(pieces, weights, bias_sum):
    model = weights[0].shape[1]
    shape = lambda rows, kind: jax.ShapeDtypeStruct((rows, model), kind)
    return pl.pallas_call(
        spread_kernel,
        out_shape=[
            shape(128, F32),
            shape(8, BF16),
            shape(72, BF16),
            shape(72, BF16),
            shape(272, BF16),
        ],
        in_specs=[WHOLE] * 9,
        out_specs=[WHOLE] * 5,
        name="spread",
        **params(16, 8 * 256 * 768 * 1024, 2 * 4 * weights[0].size),
    )(*pieces, *weights, bias_sum)


def relay_kernel(got_up, got_down, near, up, down):
    up[:64, :] = (near[:64, :].astype(F32) + got_up[:64, :].astype(F32)).astype(BF16)
    up[64:, :] = near[64:128, :]
    down[:64, :] = near[128:192, :]
    down[64:, :] = (near[192:256, :].astype(F32) + got_down[:64, :].astype(F32)).astype(BF16)


def relay(got_up, got_down, near):
    model = got_up.shape[1]
    return pl.pallas_call(
        relay_kernel,
        out_shape=[jax.ShapeDtypeStruct((128, model), BF16)] * 2,
        in_specs=[WHOLE] * 3,
        out_specs=[WHOLE] * 2,
        name="relay",
        **params(8, got_up.size, 8 * got_up.size),
    )(got_up, got_down, near)


def finish_kernel(tokens, cot, gain, out_bias, own, up, down, grad_out, layer_out):
    normed_grad = own[:64, :] + up[:64, :].astype(F32) + down[:64, :].astype(F32)
    xhat, inverse = normalise(tokens[...])
    scaled = normed_grad * gain[...]
    simple = jnp.mean(scaled, axis=-1, keepdims=True)
    product = jnp.mean(scaled * xhat, axis=-1, keepdims=True)
    grad = cot[...].astype(F32) + inverse * (scaled - simple - xhat * product)
    grad_out[...] = grad.astype(BF16)
    laid = own[64:, :] + up[64:, :].astype(F32) + down[64:, :].astype(F32)
    layer_out[...] = (tokens[...].astype(F32) + laid + out_bias[...]).astype(BF16)


def finish(tokens, cot, gain, out_bias, own, up, down):
    return pl.pallas_call(
        finish_kernel,
        out_shape=[jax.ShapeDtypeStruct(tokens.shape, BF16)] * 2,
        in_specs=[WHOLE] * 7,
        out_specs=[WHOLE] * 2,
        name="finish",
        **params(16, 20 * tokens.size, 12 * tokens.size),
    )(tokens, cot, gain, out_bias, own, up, down)


def add_kernel(factor, got, near, *refs):
    coded, out = refs[:3], refs[3]
    total = got[0].astype(F32)
    for n in range(1, got.shape[0]):
        total += got[n].astype(F32)
    height = total.shape[0]
    part = (total * factor).astype(BF16)
    rows = near[256:264, :].astype(F32)
    for ref in coded:
        rows += ref[ref.shape[0] - 8 :, :].astype(F32)
    vectors = split_rows(rows[0:1] + rows[1:2]) + split_rows(rows[2:3] + rows[3:4])
    vectors += [near[264:265, :].astype(F32), near[265:266, :].astype(F32)]
    vectors = jnp.concatenate(vectors + [jnp.zeros((2, total.shape[1]), F32)], 0)
    vectors = vectors.astype(BF16)
    for n in range(out.shape[0]):
        out[n, :height, :] = part
        out[n, height:, :] = vectors


def add(got, near, coded, factor):
    ways, height, model = got.shape
    return pl.pallas_call(
        functools.partial(add_kernel, factor),
        out_shape=jax.ShapeDtypeStruct((ways, height + 8, model), BF16),
        in_specs=[WHOLE] * 5,
        out_specs=WHOLE,
        name="add",
        **params(16, got.size, 2 * got.size),
    )(got, near, *coded)


def unpack_kernel(factor, every, qkv, out, bias, gain, shift):
    ways = every.shape[0]
    height = 4 * out.shape[0] // ways
    each = ways // 4
    total = 0
    for n in range(ways):
        rows = every[n, :height, :].astype(F32)
        here = pl.ds((n % each) * height, height)
        if n // each < 3:
            qkv[n // each, here, :] = rows
        else:
            out[here, :] = rows
        total += every[n, height:, :].astype(F32)
    total *= factor
    gain[...] = total[0:1] + total[1:2]
    shift[...] = total[2:3] + total[3:4]
    bias[...] = total[4:5] + total[5:6]


def unpack(every, width, factor):
    model = every.shape[2]
    vector = jax.ShapeDtypeStruct((1, model), F32)
    return pl.pallas_call(
        functools.partial(unpack_kernel, factor),
        out_shape=(
            jax.ShapeDtypeStruct((3, width, model), F32),
            jax.ShapeDtypeStruct((width, model), F32),
            vector,
            vector,
            vector,
        ),
        in_specs=[WHOLE],
        out_specs=(WHOLE,) * 5,
        name="unpack",
        **params(8, every.size, 6 * every.size),
    )(every)


def tie(value, *others):
    return lax.optimization_barrier((value,) + others)[0]


def on_device(
    tokens, cotangent, qkv_weight, out_weight, out_bias, norm_gain_vector, norm_bias_vector
):
    own_tokens = tokens[0]
    own_cot = cotangent[0]
    own_rows, model = own_tokens.shape
    width = qkv_weight.shape[1]
    weight = jnp.concatenate([qkv_weight.reshape(3 * width, model), out_weight], 0)
    gain = norm_gain_vector[None]
    bias = norm_bias_vector[None]
    rows = HEADS * own_rows

    right, left, cot_right, cot_left = own_tokens, own_tokens, own_cot, own_cot
    both = jnp.concatenate([own_tokens, own_cot], 0)
    norm = jnp.concatenate([gain, bias], 0)
    pieces, others = [both, to_sibling(own_tokens)], [both, to_sibling(own_cot)]
    early = None
    for steps in (1, 2, 3):
        right, left = along_z(right, 1), along_z(left, -1)
        cot_right, cot_left = along_z(cot_right, 1), along_z(cot_left, -1)
        if steps == 1:
            right, weight, norm, both = lax.optimization_barrier((right, weight, norm, both))
            pieces[0] = others[0] = both
        pieces += [right, left, to_sibling(right), to_sibling(left)]
        others += [cot_right, cot_left, to_sibling(cot_right), to_sibling(cot_left)]
        if steps == 2:
            early = project(0, pieces, others, weight, norm, rows, [])
            pieces, others = [], []
    right, cot_left = along_z(right, 1), along_z(cot_left, -1)
    right, *early = lax.optimization_barrier((right, *early))
    pieces += [right, to_sibling(right)]
    others += [cot_left, to_sibling(cot_left)]
    xhat, cot_all, own_qg, own_kv = project(
        len(EARLY) * OWN_ROWS, pieces, others, weight, norm, rows, early
    )

    other_qg = to_half(own_qg)
    arrived = [along_x(own_kv, steps) for steps in OFFSETS[:2]]
    other_qg, arrived[0], arrived[1], held_kv = lax.optimization_barrier(
        (other_qg, arrived[0], arrived[1], own_kv)
    )
    arrived.append(along_x(held_kv, OFFSETS[2]))
    own_state, own_probs, own_top = forward([own_kv], own_qg, None)
    other_state, other_probs, other_top = forward([held_kv], other_qg, None)
    first, second = order([own_qg, *own_state], [other_qg, *other_state])
    qgs = [first[0], second[0]]
    states = [first[1:], second[1:]]
    stored, tops, lses, deltas = [[], []], [[], []], [None, None], [None, None]
    got = [None, None]
    for n, wave in ((0, arrived[:2]), (1, arrived[:2]), (0, arrived[2:]), (1, arrived[2:])):
        states[n], probs, top = forward(wave, qgs[n], states[n])
        stored[n] += probs
        tops[n] += top
        if len(wave) == 1:
            got[n] = to_half(message(*states[n]))
        if n == 0:
            *states[0], qgs[1] = lax.optimization_barrier((*states[0], qgs[1]))
        elif len(wave) == 2:
            later_weight = tie(weight, states[1][0])
            w_pair, w_sib = to_pair(later_weight), to_sibling(later_weight)
            *states[1], qgs[0] = lax.optimization_barrier((*states[1], qgs[0]))

    early_att, lses[0], deltas[0] = middle(states[0], got[0], qgs[0], None)
    dqs = [None, None]
    far = (2, 0, 1)
    parts = {}
    home = []
    for n in range(2):
        if n == 1:
            got[1], dqs[0] = lax.optimization_barrier((got[1], dqs[0]))
            w_diag = to_sibling(w_pair)
            w_sib, w_pair, dqs[0] = lax.optimization_barrier((w_sib, w_pair, dqs[0]))
            att_t, lses[1], deltas[1], att = middle(states[1], got[1], qgs[1], early_att)
        for k in far:
            parts[k], dqs[n] = backward(
                None,
                arrived[k],
                stored[n][k],
                tops[n][k],
                [qgs[n]],
                [lses[n]],
                [deltas[n]],
                None if dqs[n] is None else [dqs[n]],
                None if n == 0 else parts[k],
                (F32 if n == 0 else BF16, F32),
            )
            if n == 1:
                home.append(along_x(parts[k], -OFFSETS[k]))
    own_part = None
    last = [None, None]
    for own in (False, True):
        own_part, last[own] = backward(
            own,
            own_kv,
            own_probs[0] if own else other_probs[0],
            own_top[0] if own else other_top[0],
            qgs,
            lses,
            deltas,
            dqs,
            own_part,
            (F32, F32 if own else BF16),
        )
        if not own:
            dq_part = to_half(last[0])
            home[0], own_part = lax.optimization_barrier((home[0], own_part))
    out_part, bias_sum = out_sums(tie(att_t, last[1]), cot_all)

    matrix, kept, sib, far = collect(
        last[1], dq_part, own_part, att, out_part, xhat, weight, gain, bias, home
    )
    sib, far = to_sibling(sib), to_pair(far)
    near = to_sibling(far)
    own, coded, up, down, nearest = spread(
        (kept, sib, far, near), (weight, w_sib, w_pair, w_diag), bias_sum
    )
    got_up, got_down, got_coded = along_z(up, 2), along_z(down, -2), along_z(coded, 4)
    up, down = relay(got_up, got_down, nearest)

    ways = lax.axis_size("dp") * lax.axis_size("blk")
    factor = 1.0 / math.sqrt(ways * rows)
    matrix = tie(matrix, coded).reshape(ways, 4 * width // ways, model)
    got = lax.all_to_all(matrix, ("dp", "blk"), 0, 0, tiled=True)
    back = add(got, nearest, (got_up, got_down, got_coded), factor)
    every = lax.all_to_all(back, ("dp", "blk"), 0, 0, tiled=True)
    grad_rows, layer_rows = finish(
        own_tokens, own_cot, gain, out_bias[None], own, along_z(up, 2), along_z(down, -2)
    )
    qkv_grad, out_grad, bias_grad, gain_grad, shift_grad = unpack(every, width, factor)
    return (
        layer_rows[None],
        grad_rows[None],
        qkv_grad,
        out_grad,
        bias_grad[0],
        gain_grad[0],
        shift_grad[0],
    )


def solution(mesh):
    tokens = P("dp", ("head", "blk"), None)
    heads = P("head", None)
    return jax.shard_map(
        on_device,
        mesh=mesh,
        in_specs=(tokens, tokens, P(None, "head", None), heads, P(), P(), P()),
        out_specs=(tokens, tokens, P(None, "head", None), heads, P(), P(), P()),
        check_vma=False,
    )
```

```python
import functools
import math

import jax
import jax.numpy as jnp
from jax import lax
from jax.experimental import pallas as pl
from jax.experimental.pallas import tpu as pltpu
from jax.sharding import PartitionSpec as P

HEADS = 16
EPSILON = 1e-06
ZN = 8
XN = 4
F32 = jnp.float32
BF16 = jnp.bfloat16
WHOLE = pl.BlockSpec(memory_space=pltpu.VMEM)
HBM = pl.BlockSpec(memory_space=pltpu.HBM)
NT = (((1,), (1,)), ((), ()))
TN = (((0,), (0,)), ((), ()))
NN = (((1,), (0,)), ((), ()))

OFFSETS = (1, 3, 2)

EARLY = ((0, 0), (0, 1), (-1, 0), (1, 0), (-1, 1), (1, 1), (-2, 0), (2, 0), (-2, 1), (2, 1))
LATE = ((-3, 0), (3, 0), (-3, 1), (3, 1), (4, 0), (4, 1))
OWN_ROWS = 64
PLACE = {(steps % ZN, flip): n * OWN_ROWS for n, (steps, flip) in enumerate(EARLY + LATE)}


def dot(a, b, dims=NN):
    return lax.dot_general(a, b, dims, preferred_element_type=F32)


def params(mib, flops=0, moved=0, trans=0):
    return dict(
        compiler_params=pltpu.CompilerParams(vmem_limit_bytes=mib * 2**20),
        cost_estimate=pl.CostEstimate(flops=flops, bytes_accessed=moved, transcendentals=trans),
    )


def permute(value, axis, count, target):
    return lax.ppermute(value, axis, [(i, target(i)) for i in range(count)])


def along_z(value, steps):
    return permute(value, "head", HEADS, lambda h: ((h // 2 + steps) % ZN) * 2 + h % 2)


def to_sibling(value):
    return permute(value, "head", HEADS, lambda h: h ^ 1)


def to_pair(value):
    return permute(value, "head", HEADS, lambda h: h ^ 2)


def to_diagonal(value):
    return permute(value, "head", HEADS, lambda h: h ^ 3)


def along_x(value, steps):
    return permute(value, "blk", 2 * XN, lambda b: (b // XN) * XN + (b % XN + steps) % XN)


def to_half(value):
    return permute(value, "blk", 2 * XN, lambda b: b ^ XN)


def fetch(sources, held, sems, finish_all=False):
    copies = [pltpu.make_async_copy(a, b, sems.at[n]) for n, (a, b) in enumerate(zip(sources, held))]
    for copy in copies:
        copy.start()

    if finish_all:
        for copy in copies:
            copy.wait()

    def ready(n):
        copies[n].wait()
        return held[n]

    return ready


def room(values):
    return [pltpu.VMEM(v.shape, v.dtype) for v in values] + [
        pltpu.SemaphoreType.DMA((len(values),))
    ]


def position():
    head = lax.axis_index("head")
    return head // 2, lax.rem(head, 2)


def normalise(rows):
    values = rows.astype(F32)
    shifted = values - jnp.mean(values, axis=-1, keepdims=True)
    spread = jnp.mean(shifted * shifted, axis=-1, keepdims=True)
    inverse = lax.rsqrt(spread + EPSILON)
    return shifted * inverse, inverse


def project_kernel(base, count, *refs):
    pieces, others = list(refs[:count]), list(refs[count : 2 * count])
    weight, norm = refs[2 * count : 2 * count + 2]
    gain, bias = norm[0:1, :], norm[1:2, :]
    if base == 0:
        pieces[0], others[0] = pieces[0].at[pl.ds(0, OWN_ROWS), :], others[0].at[pl.ds(OWN_ROWS, OWN_ROWS), :]
    xhat_out, cot_out, qg_out, kv_out, normed, cots = refs[-6:]
    width = weight.shape[0] // 4
    for n, piece in enumerate(pieces):
        here, there = pl.ds(n * OWN_ROWS, OWN_ROWS), pl.ds(base + n * OWN_ROWS, OWN_ROWS)
        xhat, _ = normalise(piece[...])
        xhat_out[there, :] = xhat.astype(BF16)
        normed[here, :] = (xhat * gain + bias).astype(BF16)
        cot_out[there, :] = others[n][...]
        cots[here, :] = others[n][...]
    packed = dot(normed[...], weight[: 3 * width, :], NT)
    queries = packed[:, :width].astype(BF16).astype(F32) * (1.0 / math.sqrt(width))
    there = pl.ds(base, count * OWN_ROWS)
    qg_out[there, :width] = queries.astype(BF16)
    kv_out[there, :] = packed[:, width:].astype(BF16)
    qg_out[there, width:] = dot(cots[...], weight[3 * width :, :], NT).astype(BF16)


def project(base, pieces, others, weight, norm, rows, before):
    count = len(pieces)
    total = count * OWN_ROWS
    width, model = weight.shape[0] // 4, weight.shape[1]
    first = 2 + 2 * count
    return pl.pallas_call(
        functools.partial(project_kernel, base, count),
        out_shape=(
            jax.ShapeDtypeStruct((rows, model), BF16),
            jax.ShapeDtypeStruct((rows, model), BF16),
            jax.ShapeDtypeStruct((rows, 2 * width), BF16),
            jax.ShapeDtypeStruct((rows, 2 * width), BF16),
        ),
        in_specs=[WHOLE] * (first + len(before)),
        out_specs=(WHOLE,) * 4,
        scratch_shapes=[pltpu.VMEM((total, model), BF16)] * 2,
        input_output_aliases={first + n: n for n in range(len(before))},
        name="project",
        **params(16, 2 * total * model * 4 * width, 4 * total * model * 2),
    )(*pieces, *others, weight, norm, *before)


def order_kernel(*refs):
    count = len(refs) // 4
    swap = lax.axis_index("blk") >= XN
    for n in range(count):
        own, other = refs[n][...], refs[count + n][...]
        refs[2 * count + n][...] = jnp.where(swap, other, own)
        refs[3 * count + n][...] = jnp.where(swap, own, other)


def order(own, other):
    count = len(own)
    out = pl.pallas_call(
        order_kernel,
        out_shape=[jax.ShapeDtypeStruct(v.shape, v.dtype) for v in own] * 2,
        in_specs=[WHOLE] * (2 * count),
        out_specs=[WHOLE] * (2 * count),
        name="order",
        **params(8, own[0].size, 8 * own[0].size),
    )(*own, *other)
    return out[:count], out[count:]


def forward_kernel(count, first, *refs):
    blocks = refs[:count]
    q_ref = refs[count]
    rest = refs[count + 1 :]
    if first:
        top = total = part = None
    else:
        top, total, part = rest[0][...], rest[1][...], rest[2][...]
        rest = rest[3:]
    m_out, l_out, acc_out = rest[:3]
    p_out, step_out = rest[3 : 3 + count], rest[3 + count : 3 + 2 * count]
    width = q_ref.shape[1] // 2
    queries = q_ref[:, :width]
    kvs, ahead = [], []
    for n in range(count + 1):
        if n < count:
            kvs.append(blocks[n][...])
            ahead.append(dot(kvs[n][:, :width], queries, NT))
        if n == 0:
            continue
        n, kv, scores = n - 1, kvs[n - 1], ahead[n - 1]
        new = jnp.max(scores, axis=0, keepdims=True)
        if top is not None:
            new = jnp.maximum(top, new)
        probs = jnp.exp(scores - new)
        weights = probs.astype(BF16)
        p_out[n][...] = weights
        step_out[n][...] = new
        sums = jnp.sum(probs, axis=0, keepdims=True)
        values = dot(kv[:, width:], weights, TN)
        if top is None:
            total, part = sums, values
        else:
            shrink = jnp.exp(top - new)
            total, part = total * shrink + sums, part * shrink + values
        top = new
    m_out[...], l_out[...], acc_out[...] = top, total, part


def forward(blocks, queries, state):
    count = len(blocks)
    rows, width = queries.shape[0], queries.shape[1] // 2
    keys = blocks[0].shape[0]
    first = state is None
    states = [(1, rows), (1, rows), (width, rows)]
    out = pl.pallas_call(
        functools.partial(forward_kernel, count, first),
        out_shape=[jax.ShapeDtypeStruct(s, F32) for s in states]
        + [jax.ShapeDtypeStruct((keys, rows), BF16)] * count
        + [jax.ShapeDtypeStruct((1, rows), F32)] * count,
        in_specs=[WHOLE] * (count + 1 + (0 if first else 3)),
        out_specs=[WHOLE] * (3 + 2 * count),
        name="forward",
        **params(
            24,
            count * 16 * rows * keys * width, count * 2 * rows * keys, count * rows * keys
        ),
    )(*blocks, queries, *([] if first else state))
    return out[:3], out[3 : 3 + count], out[3 + count :]


def split_thrice(value):
    high = value.astype(BF16).astype(F32)
    rest = value - high
    middle_part = rest.astype(BF16).astype(F32)
    return [high, middle_part, rest - middle_part]


def message_kernel(top, total, part, out):
    width, rows = part.shape
    out[:width, :] = part[...].astype(BF16)
    coded = split_thrice(top[...]) + split_thrice(total[...])
    coded = jnp.concatenate(coded + [jnp.zeros((10, rows), F32)], 0)
    out[width:, :] = coded.astype(BF16)


def message(top, total, part):
    width, rows = part.shape
    return pl.pallas_call(
        message_kernel,
        out_shape=jax.ShapeDtypeStruct((width + 16, rows), BF16),
        in_specs=[WHOLE] * 3,
        out_specs=WHOLE,
        name="message",
        **params(8, 4 * rows * width, 6 * rows * width),
    )(top, total, part)


def middle_kernel(top, total, part, got, qg, *refs):
    width = part.shape[0]
    earlier = refs[0] if len(refs) == 5 else None
    att_t, lse, delta = refs[1:4] if earlier is not None else refs
    coded = got[width:, :].astype(F32)
    their_top = coded[0:1] + coded[1:2] + coded[2:3]
    their_total = coded[3:4] + coded[4:5] + coded[5:6]
    new = jnp.maximum(top[...], their_top)
    mine, theirs = jnp.exp(top[...] - new), jnp.exp(their_top - new)
    both = total[...] * mine + their_total * theirs
    summed = part[...] * mine + got[:width, :].astype(F32) * theirs
    lse[...] = new + jnp.log(both)
    attended = (summed / both).astype(BF16)
    wide = attended.astype(F32)
    back = jnp.transpose(qg[:, width:].astype(F32), (1, 0))
    delta[...] = jnp.sum(back * wide, axis=0, keepdims=True)
    if earlier is not None:
        wide = jnp.where(lax.axis_index("blk") >= XN, wide, earlier[...].astype(F32))
        refs[-1][...] = jnp.transpose(wide, (1, 0)).astype(BF16)
    att_t[...] = wide.astype(BF16)


def regroup(rows, kept, sib, pair, diag):
    z, _ = position()
    width = rows.shape[1]
    for r in range(ZN // 2):
        to = pl.ds(r * OWN_ROWS, OWN_ROWS)
        for flip, near, far in ((0, kept, pair), (1, sib, diag)):
            near[to, :width] = rows[pl.ds(PLACE[2 * r, flip], OWN_ROWS), :]
            up, down = PLACE[(2 * r + 1) % ZN, flip], PLACE[(2 * r - 1) % ZN, flip]
            at = pl.multiple_of(jnp.where(lax.rem(z, 2) == 0, up, down), OWN_ROWS)
            far[to, :width] = rows[pl.ds(at, OWN_ROWS), :]


def middle(state, got, qg, earlier):
    width, rows = state[2].shape
    row = jax.ShapeDtypeStruct((1, rows), F32)
    last = earlier is not None
    att = (jax.ShapeDtypeStruct((rows, width), BF16),) if last else ()
    return pl.pallas_call(
        middle_kernel,
        out_shape=(jax.ShapeDtypeStruct((width, rows), BF16), row, row) + att,
        in_specs=[WHOLE] * (6 if last else 5),
        out_specs=(WHOLE,) * (4 if last else 3),
        name="middle",
        **params(16, 10 * rows * width, 8 * rows * width),
    )(*state, got, qg, *([earlier] if last else []))


def backward_kernel(own, has_dq, has_dkv, kv, *refs):
    count = 1 if own is None else 2
    stored, top = refs[:2]
    qgs, lses, deltas = (refs[2 + n * count : 2 + (n + 1) * count] for n in range(3))
    rest = refs[2 + 3 * count :]
    dq_in = rest[:count] if has_dq else None
    rest = rest[count:] if has_dq else rest
    dkv_in = rest[0] if has_dkv else None
    out, dq_out = rest[-2:]

    def pick(pair, *at):
        if own is None:
            return pair[0][at]
        swap = lax.axis_index("blk") >= XN
        first, second = pair if own else (pair[1], pair[0])
        return jnp.where(swap, second[at], first[at])

    width = kv.shape[1] // 2
    tile = 512
    dk = dkv_in[:, :width] if has_dkv else 0
    dv = dkv_in[:, width:] if has_dkv else 0
    for t in range(kv.shape[0] // tile):
        here = pl.ds(t * tile, tile)
        every = slice(None)
        qg = pick(qgs, here, every)
        q, grad = qg[:, :width], qg[:, width:]
        factor = jnp.exp(top[:, here] - pick(lses, every, here))
        prob_grad = dot(kv[:, width:], grad, NT)
        probs = stored[:, here].astype(F32) * factor
        score_grad = (probs * (prob_grad - pick(deltas, every, here))).astype(BF16)
        dv += dot(probs.astype(BF16), grad)
        dk += dot(score_grad, q)
        dq = dot(kv[:, :width], score_grad, TN)
        if has_dq:
            dq += pick(dq_in, every, here)
        dq_out[:, here] = dq.astype(dq_out.dtype)
    out[:, :width] = dk.astype(out.dtype)
    out[:, width:] = dv.astype(out.dtype)


def backward(own, kv, stored, top, qgs, lses, deltas, dqs, dkv, kinds):
    rows, width = qgs[0].shape[0], qgs[0].shape[1] // 2
    keys = kv.shape[0]
    given = ([] if dqs is None else list(dqs)) + ([] if dkv is None else [dkv])
    operands = [kv, stored, top, *qgs, *lses, *deltas, *given]
    return pl.pallas_call(
        functools.partial(backward_kernel, own, dqs is not None, dkv is not None),
        out_shape=[
            jax.ShapeDtypeStruct((keys, 2 * width), kinds[0]),
            jax.ShapeDtypeStruct((width, rows), kinds[1]),
        ],
        in_specs=[WHOLE] * len(operands),
        out_specs=[WHOLE] * 2,
        name="backward",
        **params(24, 32 * rows * keys * width, 2 * rows * keys),
    )(*operands)


def out_kernel(att_t, cot, part, sums):
    part[...] = dot(att_t[...], cot[...]).astype(BF16)
    sums[...] = jnp.sum(cot[...].astype(F32), axis=0, keepdims=True)


def out_sums(att_t, cot):
    return pl.pallas_call(
        out_kernel,
        out_shape=(
            jax.ShapeDtypeStruct((att_t.shape[0], cot.shape[1]), BF16),
            jax.ShapeDtypeStruct((1, cot.shape[1]), F32),
        ),
        in_specs=[WHOLE] * 2,
        out_specs=(WHOLE,) * 2,
        name="out_sums",
        **params(16, 2 * att_t.size * cot.shape[1], 2 * cot.size),
    )(att_t, cot)


def split_rows(value):
    high = value.astype(BF16).astype(F32)
    return [high, value - high]


def collect_kernel(dq, dq_part, own, att, out_part, xhat, weight, gain, bias, *refs):
    parts = refs[:3]
    grad, *targets = refs[3:7]
    wide, kept, sib, far, sems = refs[7:]
    height = kept.shape[0]
    pair, diag = far.at[pl.ds(0, height), :], far.at[pl.ds(height, height), :]
    width = dq.shape[0]
    total = own[...]
    for part in parts:
        total = total + part[...].astype(F32)
    query = dq[...] + dq_part[...].astype(F32)
    query = (query * (1.0 / math.sqrt(width))).astype(BF16).astype(F32)
    total = total.astype(BF16).astype(F32)
    packed = jnp.concatenate([jnp.transpose(query, (1, 0)), total], 1).astype(BF16)
    flipped = jnp.concatenate([query, jnp.transpose(total, (1, 0))], 0)
    wide[:, : 3 * width] = packed
    wide[:, 3 * width :] = att[...]
    regroup(wide, kept, sib, pair, diag)
    moment = dot(flipped.astype(BF16), xhat[...])
    sums = jnp.sum(flipped, axis=1, keepdims=True)
    grad[: 3 * width, :] = (moment * gain[...] + sums * bias[...]).astype(BF16)
    grad[3 * width :, :] = out_part[...]
    held = weight[: 3 * width, :].astype(F32)
    rows = split_rows(jnp.sum(held * moment, axis=0, keepdims=True))
    rows += split_rows(jnp.sum(held * sums, axis=0, keepdims=True))
    coded = [row[:, n * 256 : (n + 1) * 256] for row in rows for n in range(4)]
    coded = jnp.concatenate(coded, 0).astype(BF16)
    for target in (kept, sib, pair, diag):
        target[256:, :] = coded
    fetch((kept, sib, far), targets, sems, True)


def collect(dq, dq_part, own, att, out_part, xhat, weight, gain, bias, parts):
    width, rows = dq.shape
    quarter = jax.ShapeDtypeStruct((rows // 4 + 16, 256), BF16)
    double = jax.ShapeDtypeStruct((2 * (rows // 4 + 16), 256), BF16)
    return pl.pallas_call(
        collect_kernel,
        out_shape=(jax.ShapeDtypeStruct(weight.shape, BF16), quarter, quarter, double),
        in_specs=[WHOLE] * 12,
        out_specs=(WHOLE, HBM, HBM, HBM),
        scratch_shapes=[pltpu.VMEM((rows, 4 * width), BF16)] + room([quarter, quarter, double]),
        name="collect",
        **params(16, 8 * weight.size * rows, 24 * rows * width),
    )(dq, dq_part, own, att, out_part, xhat, weight, gain, bias, *parts)


def spread_kernel(*refs):
    bias_sum, own, vectors_out, up, down, near = refs[8:14]
    height = refs[0].shape[0]
    pieces = [refs[0], refs[1], refs[2].at[pl.ds(0, height), :], refs[3].at[pl.ds(height, height), :]]
    weights = refs[4:8]
    depth = 3 * refs[4].shape[0] // 4
    coded = sum(piece[256:, :].astype(F32) for piece in pieces)
    total = dot(
        jnp.concatenate([piece[:256, :depth] for piece in pieces], 1),
        jnp.concatenate([weight[:depth, :] for weight in weights], 0),
    )
    laid = dot(
        jnp.concatenate([piece[:256, depth:] for piece in pieces], 1),
        jnp.concatenate([weight[depth:, :] for weight in weights], 0),
    )
    vectors = []
    for v in range(2):
        row = coded[8 * v : 8 * v + 4] + coded[8 * v + 4 : 8 * v + 8]
        vectors.append(jnp.concatenate([row[n : n + 1] for n in range(4)], 1))
    rows = split_rows(vectors[0]) + split_rows(vectors[1])
    rows = jnp.concatenate(rows + [jnp.zeros((12, rows[0].shape[1]), F32)], 0).astype(BF16)
    own[:64, :], own[64:, :] = total[:64], laid[:64]
    vectors_out[...] = rows
    up[:64, :], down[:64, :] = total[128:192].astype(BF16), laid[128:192].astype(BF16)
    up[64:, :], down[64:, :] = rows, rows
    near[:64, :], near[64:128, :] = total[64:128].astype(BF16), laid[64:128].astype(BF16)
    near[128:192, :], near[192:256, :] = total[192:].astype(BF16), laid[192:].astype(BF16)
    sums = split_rows(bias_sum[...])
    sums = jnp.concatenate(sums + [jnp.zeros((14, sums[0].shape[1]), F32)], 0).astype(BF16)
    near[256:272, :], near[272:, :] = rows, sums


def spread(pieces, weights, bias_sum):
    model = weights[0].shape[1]
    shape = lambda rows, kind: jax.ShapeDtypeStruct((rows, model), kind)
    return pl.pallas_call(
        spread_kernel,
        out_shape=[
            shape(128, F32),
            shape(16, BF16),
            shape(80, BF16),
            shape(80, BF16),
            shape(288, BF16),
        ],
        in_specs=[WHOLE] * 9,
        out_specs=[WHOLE] * 5,
        name="spread",
        **params(16, 8 * 256 * 768 * 1024, 2 * 4 * weights[0].size),
    )(*pieces, *weights, bias_sum)


def relay_kernel(got_up, got_down, near, up, down):
    up[:64, :] = (near[:64, :].astype(F32) + got_up[:64, :].astype(F32)).astype(BF16)
    up[64:, :] = near[64:128, :]
    down[:64, :] = near[128:192, :]
    down[64:, :] = (near[192:256, :].astype(F32) + got_down[:64, :].astype(F32)).astype(BF16)


def relay(got_up, got_down, near):
    model = got_up.shape[1]
    return pl.pallas_call(
        relay_kernel,
        out_shape=[jax.ShapeDtypeStruct((128, model), BF16)] * 2,
        in_specs=[WHOLE] * 3,
        out_specs=[WHOLE] * 2,
        name="relay",
        **params(8, got_up.size, 8 * got_up.size),
    )(got_up, got_down, near)


def finish_kernel(tokens, cot, gain, out_bias, own, up, down, grad_out, layer_out):
    normed_grad = own[:64, :] + up[:64, :].astype(F32) + down[:64, :].astype(F32)
    xhat, inverse = normalise(tokens[...])
    scaled = normed_grad * gain[...]
    simple = jnp.mean(scaled, axis=-1, keepdims=True)
    product = jnp.mean(scaled * xhat, axis=-1, keepdims=True)
    grad = cot[...].astype(F32) + inverse * (scaled - simple - xhat * product)
    grad_out[...] = grad.astype(BF16)
    laid = own[64:, :] + up[64:, :].astype(F32) + down[64:, :].astype(F32)
    layer_out[...] = (tokens[...].astype(F32) + laid + out_bias[...]).astype(BF16)


def finish(tokens, cot, gain, out_bias, own, up, down):
    return pl.pallas_call(
        finish_kernel,
        out_shape=[jax.ShapeDtypeStruct(tokens.shape, BF16)] * 2,
        in_specs=[WHOLE] * 7,
        out_specs=[WHOLE] * 2,
        name="finish",
        **params(16, 20 * tokens.size, 12 * tokens.size),
    )(tokens, cot, gain, out_bias, own, up, down)


def add_kernel(factor, got, near, *refs):
    coded, out = refs[:3], refs[3]
    total = got[0].astype(F32)
    for n in range(1, got.shape[0]):
        total += got[n].astype(F32)
    height = total.shape[0]
    part = (total * factor).astype(BF16)
    rows = near[256:272, :].astype(F32)
    bias_rows = near[272:288, :].astype(F32)
    for ref in coded:
        rows += ref[ref.shape[0] - 16 :, :].astype(F32)
    vectors = split_rows(rows[0:1] + rows[1:2]) + split_rows(rows[2:3] + rows[3:4])
    vectors += [bias_rows[0:1], bias_rows[1:2]]
    vectors = jnp.concatenate(vectors + [jnp.zeros((2, total.shape[1]), F32)], 0)
    vectors = vectors.astype(BF16)
    for n in range(out.shape[0]):
        out[n, :height, :] = part
        out[n, height:, :] = vectors


def add(got, near, coded, factor):
    ways, height, model = got.shape
    return pl.pallas_call(
        functools.partial(add_kernel, factor),
        out_shape=jax.ShapeDtypeStruct((ways, height + 8, model), BF16),
        in_specs=[WHOLE] * 5,
        out_specs=WHOLE,
        name="add",
        **params(16, got.size, 2 * got.size),
    )(got, near, *coded)


def unpack_kernel(factor, every, qkv, out, bias, gain, shift):
    ways = every.shape[0]
    height = 4 * out.shape[0] // ways
    each = ways // 4
    total = 0
    for n in range(ways):
        rows = every[n, :height, :].astype(F32)
        here = pl.ds((n % each) * height, height)
        if n // each < 3:
            qkv[n // each, here, :] = rows
        else:
            out[here, :] = rows
        total += every[n, height:, :].astype(F32)
    total *= factor
    gain[...] = total[0:1] + total[1:2]
    shift[...] = total[2:3] + total[3:4]
    bias[...] = total[4:5] + total[5:6]


def unpack(every, width, factor):
    model = every.shape[2]
    vector = jax.ShapeDtypeStruct((1, model), F32)
    return pl.pallas_call(
        functools.partial(unpack_kernel, factor),
        out_shape=(
            jax.ShapeDtypeStruct((3, width, model), F32),
            jax.ShapeDtypeStruct((width, model), F32),
            vector,
            vector,
            vector,
        ),
        in_specs=[WHOLE],
        out_specs=(WHOLE,) * 5,
        name="unpack",
        **params(8, every.size, 6 * every.size),
    )(every)


def tie(value, *others):
    return lax.optimization_barrier((value,) + others)[0]


def on_device(
    tokens, cotangent, qkv_weight, out_weight, out_bias, norm_gain_vector, norm_bias_vector
):
    own_tokens = tokens[0]
    own_cot = cotangent[0]
    own_rows, model = own_tokens.shape
    width = qkv_weight.shape[1]
    weight = jnp.concatenate([qkv_weight.reshape(3 * width, model), out_weight], 0)
    gain = norm_gain_vector[None]
    bias = norm_bias_vector[None]
    rows = HEADS * own_rows

    right, left, cot_right, cot_left = own_tokens, own_tokens, own_cot, own_cot
    both = jnp.concatenate([own_tokens, own_cot], 0)
    norm = jnp.concatenate([gain, bias], 0)
    pieces, others = [both, to_sibling(own_tokens)], [both, to_sibling(own_cot)]
    early = None
    for steps in (1, 2, 3):
        right, left = along_z(right, 1), along_z(left, -1)
        cot_right, cot_left = along_z(cot_right, 1), along_z(cot_left, -1)
        if steps == 1:
            right, weight, norm, both = lax.optimization_barrier((right, weight, norm, both))
            pieces[0] = others[0] = both
        pieces += [right, left, to_sibling(right), to_sibling(left)]
        others += [cot_right, cot_left, to_sibling(cot_right), to_sibling(cot_left)]
        if steps == 2:
            early = project(0, pieces, others, weight, norm, rows, [])
            pieces, others = [], []
    right, cot_left = along_z(right, 1), along_z(cot_left, -1)
    right, *early = lax.optimization_barrier((right, *early))
    pieces += [right, to_sibling(right)]
    others += [cot_left, to_sibling(cot_left)]
    xhat, cot_all, own_qg, own_kv = project(
        len(EARLY) * OWN_ROWS, pieces, others, weight, norm, rows, early
    )

    other_qg = to_half(own_qg)
    arrived = [along_x(own_kv, steps) for steps in OFFSETS[:2]]
    other_qg, arrived[0], arrived[1], held_kv = lax.optimization_barrier(
        (other_qg, arrived[0], arrived[1], own_kv)
    )
    arrived.append(along_x(held_kv, OFFSETS[2]))
    own_state, own_probs, own_top = forward([own_kv], own_qg, None)
    other_state, other_probs, other_top = forward([held_kv], other_qg, None)
    first, second = order([own_qg, *own_state], [other_qg, *other_state])
    qgs = [first[0], second[0]]
    states = [first[1:], second[1:]]
    stored, tops, lses, deltas = [[], []], [[], []], [None, None], [None, None]
    got = [None, None]
    for n, wave in ((0, arrived[:2]), (1, arrived[:2]), (0, arrived[2:]), (1, arrived[2:])):
        states[n], probs, top = forward(wave, qgs[n], states[n])
        stored[n] += probs
        tops[n] += top
        if len(wave) == 1:
            got[n] = to_half(message(*states[n]))
        if n == 0:
            *states[0], qgs[1] = lax.optimization_barrier((*states[0], qgs[1]))
        elif len(wave) == 2:
            later_weight = tie(weight, states[1][0])
            w_pair, w_sib = to_pair(later_weight), to_sibling(later_weight)
            *states[1], qgs[0] = lax.optimization_barrier((*states[1], qgs[0]))

    early_att, lses[0], deltas[0] = middle(states[0], got[0], qgs[0], None)
    dqs = [None, None]
    far = (2, 0, 1)
    parts = {}
    home = []
    for n in range(2):
        if n == 1:
            got[1], dqs[0] = lax.optimization_barrier((got[1], dqs[0]))
            w_diag = to_sibling(w_pair)
            w_sib, w_pair, dqs[0] = lax.optimization_barrier((w_sib, w_pair, dqs[0]))
            att_t, lses[1], deltas[1], att = middle(states[1], got[1], qgs[1], early_att)
        for k in far:
            parts[k], dqs[n] = backward(
                None,
                arrived[k],
                stored[n][k],
                tops[n][k],
                [qgs[n]],
                [lses[n]],
                [deltas[n]],
                None if dqs[n] is None else [dqs[n]],
                None if n == 0 else parts[k],
                (F32 if n == 0 else BF16, F32),
            )
            if n == 1:
                home.append(along_x(parts[k], -OFFSETS[k]))
    own_part = None
    last = [None, None]
    for own in (False, True):
        own_part, last[own] = backward(
            own,
            own_kv,
            own_probs[0] if own else other_probs[0],
            own_top[0] if own else other_top[0],
            qgs,
            lses,
            deltas,
            dqs,
            own_part,
            (F32, F32 if own else BF16),
        )
        if not own:
            dq_part = to_half(last[0])
            home[0], own_part = lax.optimization_barrier((home[0], own_part))
    out_part, bias_sum = out_sums(tie(att_t, last[1]), cot_all)

    matrix, kept, sib, far = collect(
        last[1], dq_part, own_part, att, out_part, xhat, weight, gain, bias, home
    )
    sib, far = to_sibling(sib), to_pair(far)
    near = to_sibling(far)
    own, coded, up, down, nearest = spread(
        (kept, sib, far, near), (weight, w_sib, w_pair, w_diag), bias_sum
    )
    got_up, got_down, got_coded = along_z(up, 2), along_z(down, -2), along_z(coded, 4)
    up, down = relay(got_up, got_down, nearest)

    ways = lax.axis_size("dp") * lax.axis_size("blk")
    factor = 1.0 / math.sqrt(ways * rows)
    matrix = tie(matrix, coded).reshape(ways, 4 * width // ways, model)
    got = lax.all_to_all(matrix, ("dp", "blk"), 0, 0, tiled=True)
    back = add(got, nearest, (got_up, got_down, got_coded), factor)
    every = lax.all_to_all(back, ("dp", "blk"), 0, 0, tiled=True)
    grad_rows, layer_rows = finish(
        own_tokens, own_cot, gain, out_bias[None], own, along_z(up, 2), along_z(down, -2)
    )
    qkv_grad, out_grad, bias_grad, gain_grad, shift_grad = unpack(every, width, factor)
    return (
        layer_rows[None],
        grad_rows[None],
        qkv_grad,
        out_grad,
        bias_grad[0],
        gain_grad[0],
        shift_grad[0],
    )


def solution(mesh):
    tokens = P("dp", ("head", "blk"), None)
    heads = P("head", None)
    return jax.shard_map(
        on_device,
        mesh=mesh,
        in_specs=(tokens, tokens, P(None, "head", None), heads, P(), P(), P()),
        out_specs=(tokens, tokens, P(None, "head", None), heads, P(), P(), P()),
        check_vma=False,
    )
```
